128 devices in a mesh: dp: 4 (over z), cp: 32 (over y, x, core).
Axes of the slice: x: 4, y: 4, z: 4, core: 2. Of those that a mesh axis runs over, the one named last changes fastest.
Arguments:
- pre_q_nope: bfloat16 [8192, 8192], P('cp', 'dp'), may hold values from -3 to 3
- pre_q_rope: bfloat16 [8192, 4096], P('cp', 'dp'), may hold values from -8 to 8
- pre_latent: bfloat16 [8192, 512], P('cp'), may hold values from -6 to 6
- pre_rope: bfloat16 [8192, 64], P('cp'), may hold values from -8 to 8
- up_keys: bfloat16 [64, 128, 512], P('dp'), may hold values from -0.5 to 0.5
- up_values: bfloat16 [64, 512, 128], P('dp'), may hold values from -1.1953125 to 1.1953125
- new_lengths: int32 [8], replicated, may hold values from 1 to 32, as said below
- new_hosts: int32 [8], replicated, may hold values from 0 to 127, as said below
- req_pages: int32 [1024, 32], P(('dp', 'cp')), may hold values from 0 to 95, as said below
- req_len: int32 [1024], P(('dp', 'cp')), may hold values from 1 to 2048, as said below
- row_request: int32 [128, 8], P(('dp', 'cp')), may hold values from 0 to 7, each once within a row
- cache_latent: bfloat16 [524288, 512], P(('dp', 'cp')), may hold values from -6 to 6
- cache_rope: bfloat16 [524288, 64], P(('dp', 'cp')), may hold values from -6 to 6
- dec_q_nope: bfloat16 [3, 1024, 8192], P(None, ('dp', 'cp')), may hold values from -3 to 3
- dec_q_rope: bfloat16 [3, 1024, 4096], P(None, ('dp', 'cp')), may hold values from -8 to 8
- new_latent: bfloat16 [3, 1024, 512], P(None, ('dp', 'cp')), may hold values from -6 to 6
- new_rope: bfloat16 [3, 1024, 64], P(None, ('dp', 'cp')), may hold values from -8 to 8
Outputs:
- prefill_out: bfloat16 [8192, 8192], P('cp', 'dp')
- decode_out: bfloat16 [3, 1024, 8192], P(None, ('dp', 'cp'))
The draws below stay inside these ranges and needn't reach their ends.
Inputs may be any that keep to these rules, and one draw needn't show every extreme that they name: `new_lengths`: pages of each new request, in the order of the prefill stream; they sum to 128, and one request has 32. `new_hosts`: the device, numbered dp index times the size of cp plus cp index, that hosts each new request; no two alike. `req_pages`: the 32 pool pages of each request slot of a device, in order; pool pages 64 and up hold what arrives for a new request: the first slot of a hosting device lists exactly them in order, and no other slot names them. `req_len`: the first slot of a hosting device has 64 times its new request's pages; the second slot of every device has 2048, the third 1. `row_request`: each device's decode rows name each of its request slots once.
All inputs are finite; a program needn't handle non-finite values.
Results may differ from the reference program's by a relative error of at most 0.015.
Values may be sent and summed in bfloat16 or wider, within the bound.
A program may use at most 192 MiB of HBM per device.

```python
import jax
import jax.numpy as jnp
from jax import lax

H = 64
DN = 128
DR = 64
DL = 512
DV = 128
PAGE = 64
NSTEP = 3
NREQ = 8
REQ_DEV = 8
OLD_DEV = 64
TOKENS_P = 8192
LMAXP = 32
N_DP = 4
N_CP = 32


def new_requests(key):
    middle = LMAXP // 2
    device_count = N_DP * N_CP
    key_lengths, key_order, key_hosts = jax.random.split(key, 3)
    offsets = jax.random.randint(key_lengths, (NREQ // 2,), 1 - middle, middle)
    offsets = offsets.at[0].set(middle - 1)
    offsets = offsets.at[1].set(jnp.maximum(offsets[1], 2 - middle))
    paired = jnp.stack([middle + offsets, middle - offsets], axis=1).reshape(NREQ)
    paired = paired.at[0].add(1).at[2].add(-1)
    lengths = paired[jax.random.permutation(key_order, NREQ)]
    chosen = jax.random.permutation(key_hosts, device_count)[:NREQ]
    present = jnp.any(chosen == device_count - 1)
    chosen = chosen.at[0].set(jnp.where(present, chosen[0], device_count - 1))
    return (lengths.astype(jnp.int32), chosen.astype(jnp.int32))


def host_table(lengths, chosen):
    device_count = N_DP * N_CP
    hits = (chosen[None, :] == jnp.arange(device_count, dtype=jnp.int32)[:, None]).astype(jnp.int32)
    is_host = jnp.sum(hits, axis=1) > 0
    new_tokens = jnp.sum(hits * lengths[None, :], axis=1) * PAGE
    return (is_host, new_tokens)


def draw_new_lengths(key, part):
    lengths, chosen = new_requests(key)
    return lengths


def draw_new_hosts(key, part):
    lengths, chosen = new_requests(key)
    return chosen


def draw_req_pages(key, part):
    lengths, chosen = new_requests(key)
    key = jax.random.fold_in(key, 5)
    is_host, new_tokens = host_table(lengths, chosen)
    listed = jax.random.randint(key, (N_DP * N_CP, REQ_DEV, LMAXP), 0, OLD_DEV)
    arrived = OLD_DEV + jnp.arange(LMAXP, dtype=jnp.int32)
    leading = jnp.where(is_host[:, None], arrived[None, :], listed[:, 0, :])
    listed = listed.at[:, 0, :].set(leading)
    return listed.reshape(N_DP * N_CP * REQ_DEV, LMAXP).astype(jnp.int32)


def draw_req_len(key, part):
    lengths, chosen = new_requests(key)
    key = jax.random.fold_in(key, 6)
    is_host, new_tokens = host_table(lengths, chosen)
    counts = jax.random.randint(key, (N_DP * N_CP, REQ_DEV), 1, LMAXP * PAGE + 1)
    counts = counts.at[:, 1].set(LMAXP * PAGE)
    counts = counts.at[:, 2].set(1)
    counts = counts.at[:, 0].set(jnp.where(is_host, new_tokens, counts[:, 0]))
    return counts.reshape(N_DP * N_CP * REQ_DEV).astype(jnp.int32)


def loud_rows(key, count, boost):
    key_pick, key_sign, key_size = jax.random.split(key, 3)
    picked = jax.random.randint(key_pick, (count,), 0, 23) == 0
    signs = jax.random.rademacher(key_sign, (count, DR), dtype=jnp.float32)
    strength = jax.random.uniform(key_size, (count, 1), minval=1.0, maxval=1.45)
    loudness = 5.0 * signs * strength
    picked = jnp.logical_and(picked, boost > 0.5)
    return (picked, loudness)


def prefill_keys(key, boost):
    base = jnp.clip(jax.random.normal(jax.random.fold_in(key, 100), (TOKENS_P, DR), dtype=jnp.float32), -6.0, 6.0)
    picked, loudness = loud_rows(jax.random.fold_in(key, 101), TOKENS_P, boost)
    echoed = jnp.roll(picked, 1).at[0].set(False)
    marked = jnp.logical_and(echoed, jnp.logical_not(picked))
    earlier = jnp.roll(loudness, 1, axis=0)
    table = jnp.where(picked[:, None], loudness, base)
    table = jnp.where(marked[:, None], 0.99 * earlier, table)
    return (table, marked, earlier)


def draw_pre_rope(key, part):
    boost = 0.0
    table, marked, earlier = prefill_keys(key, boost)
    return table.astype(jnp.bfloat16)


def draw_pre_q_rope(key, part):
    boost = 0.0
    table, marked, earlier = prefill_keys(key, boost)
    key = jax.random.fold_in(key, 7)
    queries = jnp.clip(jax.random.normal(key, (TOKENS_P, H, DR), dtype=jnp.float32), -6.0, 6.0)
    queries = jnp.where(marked[:, None, None], earlier[:, None, :], queries)
    return queries.reshape(TOKENS_P, H * DR).astype(jnp.bfloat16)


def decode_keys(key, boost):
    every_row = N_DP * N_CP * REQ_DEV
    base = jnp.clip(jax.random.normal(jax.random.fold_in(key, 200), (NSTEP, every_row, DR), dtype=jnp.float32), -6.0, 6.0)
    picked, loudness = loud_rows(jax.random.fold_in(key, 201), every_row, boost)
    fading = 0.99 ** jnp.arange(NSTEP, dtype=jnp.float32)
    aligned = fading[:, None, None] * loudness[None, :, :]
    table = jnp.where(picked[None, :, None], aligned, base)
    return (table, picked, aligned)


def draw_new_rope(key, part):
    boost = 0.0
    table, picked, aligned = decode_keys(key, boost)
    return table.astype(jnp.bfloat16)


def draw_dec_q_rope(key, part):
    boost = 0.0
    table, picked, aligned = decode_keys(key, boost)
    key = jax.random.fold_in(key, 8)
    every_row = N_DP * N_CP * REQ_DEV
    queries = jnp.clip(jax.random.normal(key, (NSTEP, every_row, H, DR), dtype=jnp.float32), -6.0, 6.0)
    queries = jnp.where(picked[None, :, None, None], aligned[:, :, None, :], queries)
    return queries.reshape(NSTEP, every_row, H * DR).astype(jnp.bfloat16)


def steps_of(stream_key, shape, cuts, low, top_value):
    level, own = 1.0, jax.random.fold_in(stream_key, 6)
    for dim, blocks in cuts:
        heights = jnp.exp(jax.random.uniform(jax.random.fold_in(own, dim), (blocks,), jnp.float32, low / len(cuts), top_value / len(cuts)))
        level = level * jnp.repeat(heights, shape[dim] // blocks).reshape([-1 if axis == dim else 1 for axis in range(len(shape))])
    return level


def noise(key, shape, width, limit, cuts=(), kind=jnp.bfloat16):
    gain = steps_of(key, shape, cuts, -0.22, 0.18) if cuts else 1.0
    entries = jax.random.normal(key, shape, jnp.float32) * width * gain
    return jnp.minimum(jnp.maximum(entries, -limit), limit).astype(kind)


def setup_inputs(seed: int = 0) -> dict:
    arg_keys = jax.random.split(jax.random.key(seed), 18)
    return {
        "pre_q_nope": noise(arg_keys[0], (TOKENS_P, H * DN), 0.5, 3.0, ((0, 32), (1, 4))),
        "pre_q_rope": draw_pre_q_rope(jax.random.fold_in(arg_keys[17], 71), 0),
        "pre_latent": noise(arg_keys[2], (TOKENS_P, DL), 1.0, 6.0, ((0, 32),)),
        "pre_rope": draw_pre_rope(jax.random.fold_in(arg_keys[17], 71), 0),
        "up_keys": noise(arg_keys[4], (H, DN, DL), DN ** -0.5, 0.5, ((0, 4),)),
        "up_values": noise(arg_keys[5], (H, DL, DV), 0.2, 1.1953125, ((0, 4),)),
        "new_lengths": draw_new_lengths(jax.random.fold_in(arg_keys[17], 71), 0),
        "new_hosts": draw_new_hosts(jax.random.fold_in(arg_keys[17], 71), 0),
        "req_pages": draw_req_pages(jax.random.fold_in(arg_keys[17], 71), 0),
        "req_len": draw_req_len(jax.random.fold_in(arg_keys[17], 71), 0),
        "row_request": jax.vmap(lambda own: jax.random.permutation(own, REQ_DEV))(jax.random.split(arg_keys[10], (N_DP * N_CP))).reshape((N_DP * N_CP, REQ_DEV)).astype(jnp.int32),
        "cache_latent": noise(arg_keys[11], (N_DP * N_CP * OLD_DEV * PAGE, DL), 1.0, 6.0, ((0, 128),)),
        "cache_rope": noise(arg_keys[12], (N_DP * N_CP * OLD_DEV * PAGE, DR), 1.0, 6.0, ((0, 128),)),
        "dec_q_nope": noise(arg_keys[13], (NSTEP, N_DP * N_CP * REQ_DEV, H * DN), 0.5, 3.0, ((1, 128),)),
        "dec_q_rope": draw_dec_q_rope(jax.random.fold_in(arg_keys[17], 71), 0),
        "new_latent": noise(arg_keys[15], (NSTEP, N_DP * N_CP * REQ_DEV, DL), 1.0, 6.0, ((1, 128),)),
        "new_rope": draw_new_rope(jax.random.fold_in(arg_keys[17], 71), 0),
    }


NEGATIVE = -1e30


def request_of(lengths, offset, count):
    starts = ((jnp.cumsum(lengths) - lengths) * PAGE).astype(jnp.int32)
    places = offset + jnp.arange(count, dtype=jnp.int32)
    return jnp.sum((places[:, None] >= starts[None, :]).astype(jnp.int32), axis=1) - 1


def masked_softmax(scores, allowed):
    scores = jnp.where(allowed, scores, NEGATIVE)
    summit = jnp.max(scores, axis=-1, keepdims=True)
    raised = jnp.where(allowed, jnp.exp(scores - summit), 0.0)
    return (raised / jnp.sum(raised, axis=-1, keepdims=True)).astype(jnp.bfloat16)


def prefill(pre_q_nope, pre_q_rope, pre_latent, pre_rope, up_keys, up_values, new_lengths):
    length = pre_latent.shape[0]
    scaling = (DN + DR) ** -0.5
    request_span = LMAXP * PAGE
    queries = jnp.einsum("thd,hdl->thl", pre_q_nope.reshape(length, H, DN).astype(jnp.float32), up_keys.astype(jnp.float32)).astype(jnp.bfloat16)
    rotary = pre_q_rope.reshape(length, H, DR).astype(jnp.float32)
    owners = request_of(new_lengths, 0, length)
    block_rows = min(512, length)
    results = []
    for opening in range(0, length, block_rows):
        lowest = max(0, opening - request_span)
        closing = opening + block_rows
        window = pre_latent[lowest:closing].astype(jnp.float32)
        window_rope = pre_rope[lowest:closing].astype(jnp.float32)
        scores = (jnp.einsum("thl,jl->htj", queries[opening:closing].astype(jnp.float32), window)
                  + jnp.einsum("thr,jr->htj", rotary[opening:closing], window_rope)) * scaling
        query_pos = jnp.arange(opening, closing, dtype=jnp.int32)
        key_pos = jnp.arange(lowest, closing, dtype=jnp.int32)
        allowed = (owners[opening:closing][:, None] == owners[lowest:closing][None, :]) & (key_pos[None, :] <= query_pos[:, None])
        weights = masked_softmax(scores, allowed[None])
        latent_out = jnp.einsum("htj,jl->thl", weights.astype(jnp.float32), window).astype(jnp.bfloat16)
        expanded = jnp.einsum("thl,hlv->thv", latent_out.astype(jnp.float32), up_values.astype(jnp.float32)).astype(jnp.bfloat16)
        results.append(expanded.reshape(closing - opening, H * DV))
    return jnp.concatenate(results, axis=0)


def decode_attend(queries, query_rope, keys_latent, keys_rope, usable, fresh_latent, fresh_rope):
    scaling = (DN + DR) ** -0.5
    step_count = queries.shape[0]
    queries = queries.astype(jnp.float32)
    query_rope = query_rope.astype(jnp.float32)
    keys_latent = keys_latent.astype(jnp.float32)
    fresh_latent = fresh_latent.astype(jnp.float32)
    cached = (jnp.einsum("srhl,rkl->srhk", queries, keys_latent)
              + jnp.einsum("srhe,rke->srhk", query_rope, keys_rope.astype(jnp.float32))) * scaling
    recent = (jnp.einsum("srhl,trl->srht", queries, fresh_latent)
              + jnp.einsum("srhe,tre->srht", query_rope, fresh_rope.astype(jnp.float32))) * scaling
    cache_mask = usable[None, :, None, :]
    steps_seen = jnp.arange(step_count, dtype=jnp.int32)
    recent_mask = (steps_seen[None, :] <= steps_seen[:, None])[:, None, None, :]
    cached = jnp.where(cache_mask, cached, NEGATIVE)
    recent = jnp.where(recent_mask, recent, NEGATIVE)
    summit = jnp.maximum(jnp.max(cached, axis=-1, keepdims=True), jnp.max(recent, axis=-1, keepdims=True))
    cached_exp = jnp.where(cache_mask, jnp.exp(cached - summit), 0.0)
    recent_exp = jnp.where(recent_mask, jnp.exp(recent - summit), 0.0)
    denominator = jnp.sum(cached_exp, axis=-1, keepdims=True) + jnp.sum(recent_exp, axis=-1, keepdims=True)
    cached_weights = (cached_exp / denominator).astype(jnp.bfloat16)
    recent_weights = (recent_exp / denominator).astype(jnp.bfloat16)
    gathered = (jnp.einsum("srhk,rkl->srhl", cached_weights.astype(jnp.float32), keys_latent)
                + jnp.einsum("srht,trl->srhl", recent_weights.astype(jnp.float32), fresh_latent))
    return gathered.astype(jnp.bfloat16)


def decode_device(device, cache_part, cache_rope_part, pages, token_counts, rows_map, query_nope, query_rope,
                  fresh_latent, fresh_rope, padded_latent, padded_rope, new_lengths, new_hosts, up_keys, up_values):
    request_span = LMAXP * PAGE
    starts = (jnp.cumsum(new_lengths) - new_lengths).astype(jnp.int32)
    arrival = jnp.sum(jnp.where(new_hosts == device, starts, 0)).astype(jnp.int32) * PAGE
    arrived = lax.dynamic_slice_in_dim(padded_latent, arrival, request_span, 0)
    arrived_rope = lax.dynamic_slice_in_dim(padded_rope, arrival, request_span, 0)
    pool_latent = jnp.concatenate([cache_part, arrived], axis=0)
    pool_rope = jnp.concatenate([cache_rope_part, arrived_rope], axis=0)
    slot_count = rows_map.shape[0]
    picker = (rows_map[:, None] == jnp.arange(slot_count, dtype=jnp.int32)[None, :]).astype(jnp.int32)
    row_pages = jnp.sum(picker[:, :, None] * pages[None, :, :], axis=1)
    row_counts = jnp.sum(picker * token_counts[None, :], axis=1)
    token_index = (row_pages[:, :, None] * PAGE + jnp.arange(PAGE, dtype=jnp.int32)[None, None, :]).reshape(slot_count, request_span)
    keys_latent = pool_latent[token_index]
    keys_rope = pool_rope[token_index]
    usable = jnp.arange(request_span, dtype=jnp.int32)[None, :] < row_counts[:, None]
    step_count = query_nope.shape[0]
    queries = jnp.einsum("srhd,hdl->srhl", query_nope.reshape(step_count, slot_count, H, DN).astype(jnp.float32),
                         up_keys.astype(jnp.float32)).astype(jnp.bfloat16)
    rotary = query_rope.reshape(step_count, slot_count, H, DR)
    latent_out = decode_attend(queries, rotary, keys_latent, keys_rope, usable, fresh_latent, fresh_rope)
    expanded = jnp.einsum("srhl,hlv->srhv", latent_out.astype(jnp.float32), up_values.astype(jnp.float32)).astype(jnp.bfloat16)
    return expanded.reshape(step_count, slot_count, H * DV)


def reference(pre_q_nope, pre_q_rope, pre_latent, pre_rope, up_keys, up_values, new_lengths, new_hosts,
              req_pages, req_len, row_request, cache_latent, cache_rope, dec_q_nope, dec_q_rope, new_latent, new_rope):
    prefill_out = prefill(pre_q_nope, pre_q_rope, pre_latent, pre_rope, up_keys, up_values, new_lengths)
    device_count = N_DP * N_CP
    request_span = LMAXP * PAGE
    padded_latent = jnp.concatenate([pre_latent, jnp.zeros((request_span, DL), pre_latent.dtype)], axis=0)
    padded_rope = jnp.concatenate([pre_rope, jnp.zeros((request_span, DR), pre_rope.dtype)], axis=0)
    device_ids = jnp.arange(device_count, dtype=jnp.int32)
    cache_parts = cache_latent.reshape(device_count, OLD_DEV * PAGE, DL)
    cache_rope_parts = cache_rope.reshape(device_count, OLD_DEV * PAGE, DR)
    page_parts = req_pages.reshape(device_count, REQ_DEV, LMAXP)
    count_parts = req_len.reshape(device_count, REQ_DEV)
    nope_parts = jnp.transpose(dec_q_nope.reshape(NSTEP, device_count, REQ_DEV, H * DN), (1, 0, 2, 3))
    rope_parts = jnp.transpose(dec_q_rope.reshape(NSTEP, device_count, REQ_DEV, H * DR), (1, 0, 2, 3))
    fresh_parts = jnp.transpose(new_latent.reshape(NSTEP, device_count, REQ_DEV, DL), (1, 0, 2, 3))
    fresh_rope_parts = jnp.transpose(new_rope.reshape(NSTEP, device_count, REQ_DEV, DR), (1, 0, 2, 3))

    def one_device(packed):
        return decode_device(packed[0], packed[1], packed[2], packed[3], packed[4], packed[5], packed[6], packed[7],
                             packed[8], packed[9], padded_latent, padded_rope, new_lengths, new_hosts, up_keys, up_values)

    outputs = lax.map(one_device, (device_ids, cache_parts, cache_rope_parts, page_parts, count_parts, row_request,
                                   nope_parts, rope_parts, fresh_parts, fresh_rope_parts))
    decode_out = jnp.transpose(outputs, (1, 0, 2, 3)).reshape(NSTEP, device_count * REQ_DEV, H * DV)
    return prefill_out, decode_out
```

```python
import jax
import jax.numpy as jnp
from jax import lax
from jax.experimental import pallas as pl
from jax.experimental.pallas import tpu as pltpu
from jax.sharding import PartitionSpec as P

DN, DR, DL, DV, PAGE = 128, 64, 512, 128, 64
F32, BF = jnp.float32, jnp.bfloat16
SCALE = (DN + DR) ** -0.5 * 1.4426950408889634
NEG = -1e30
KW = DL + 2 * DR
CHUNK = 768
MESH = pl.DeviceIdType.MESH


def nt(a, b):
    return lax.dot_general(a, b, (((1,), (1,)), ((), ())), preferred_element_type=F32)


def nn(a, b):
    return lax.dot_general(a, b, (((1,), (0,)), ((), ())), preferred_element_type=F32)


def half_lanes(pair, odd):
    lane = lax.broadcasted_iota(jnp.int32, pair.shape, 1)
    return jnp.where((lane >= DR) if odd else (lane < DR), pair, jnp.zeros_like(pair))


def kernel(
    lengths, hosts, pages, counts, row_slot,
    qn_h, qr_h, lat_h, rope_h, upk_h, upv_h, cl_h, cr_h, dq_h, dqr_h, nl_h, nr_h,
    pout_h, dout_h,
    allb, rope_st, pool, cr_st, upk, upv, qn, qr, pout, bias,
    qx, dqr, nl, nr, flip, qsend, qrecv, qrope, fresh, obuf, orecv, ysend, yrecv, dout,
    load_sem, z_send, z_recv, q_send, q_recv, o_send, o_recv, y_send, y_recv,
    a_send, a_recv, out_sem,
):
    z = lax.axis_index("dp")
    c = lax.axis_index("cp")
    core = lax.rem(c, 2)
    chip = lax.div(c, 2)
    cx, cy = lax.rem(chip, 4), lax.div(chip, 4)
    a = cx + core * (cy - cx)
    b = cy + core * (cx - cy)

    def at(da, db):
        pa, pb = lax.rem(a + da + 4, 4), lax.rem(b + db + 4, 4)
        return 2 * (pa * (1 + 3 * core) + pb * (4 - 3 * core)) + core

    sibling = c + 1 - 2 * core
    zp = [lax.rem(z + d, 4) for d in range(4)]

    loads = [
        (lat_h, allb.at[pl.ds(4 * c, 4), :, pl.ds(0, DL)]),
        (rope_h, rope_st),
        (dq_h.at[:, :, pl.ds(pl.multiple_of(z * 2048, 2048), 2048)], qx.at[z]),
        (upk_h, upk),
        (dqr_h, dqr),
        (nl_h, nl),
        (nr_h, nr),
        (cl_h, pool.at[:, :, pl.ds(0, DL)]),
        (cr_h, cr_st),
        (qn_h, qn),
        (qr_h, qr),
        (upv_h, upv),
    ]
    loads = [pltpu.make_async_copy(s, d, load_sem.at[i]) for i, (s, d) in enumerate(loads)]
    for one in loads:
        one.start()

    barrier = pltpu.get_barrier_semaphore()
    peers = [(z, at(1, 0)), (z, at(-1, 0)), (z, at(0, 1)), (z, at(0, -1)), (z, sibling)]
    peers += [(zp[d], c) for d in (1, 2, 3)]
    for peer in peers:
        pl.semaphore_signal(barrier, inc=1, device_id=peer, device_id_type=MESH)
    pl.semaphore_wait(barrier, len(peers))

    def remote(src, dst, send, recv, peer):
        return pltpu.make_async_remote_copy(
            src_ref=src, dst_ref=dst, send_sem=send, recv_sem=recv,
            device_id=peer, device_id_type=MESH)

    z_copies = []
    for d in (1, 2, 3):
        cols = pl.ds(pl.multiple_of(zp[d] * 2048, 2048), 2048)
        z_copies.append(remote(dq_h.at[:, :, cols], qx.at[z], z_send.at[d], z_recv.at[d], (zp[d], c)))
        z_copies[-1].start()

    loads[0].wait()
    loads[1].wait()
    own_rope = rope_st[...]
    allb[pl.ds(4 * c, 4), :, DL:] = jnp.concatenate([own_rope, own_rope], axis=2)

    def rows(block, half=None):
        if half is None:
            return allb.at[pl.ds(block * 4, 4)]
        return allb.at[pl.ds(block * 4 + half * 2, 2)]

    gather = {}
    slots = [0]

    def push(key, da, db, pa, pb, half=None):
        i = slots[0]
        slots[0] += 1
        ref = rows(at(da, db), half)
        copy = remote(ref, ref, a_send.at[i], a_recv.at[i], (z, at(pa, pb)))
        copy.start()
        gather[key] = copy

    def share(da, db):
        i = slots[0]
        slots[0] += 1
        ref = rows(at(da, db))
        copy = remote(ref, ref, a_send.at[i], a_recv.at[i], (z, sibling))
        copy.start()
        gather["s", da, db] = copy

    def got(*key):
        gather[key].wait_recv()

    push(("a", -1), 0, 0, 1, 0)
    push(("a", 1), 0, 0, -1, 0)
    push(("b", 0, -1), 0, 0, 0, 1)
    push(("b", 0, 1), 0, 0, 0, -1)
    share(0, 0)

    starts = [jnp.int32(0)]
    for r in range(7):
        starts.append(starts[-1] + lengths[r] * PAGE)
    query_pos = c * 256 + lax.broadcasted_iota(jnp.int32, (256, CHUNK), 0)
    low = jnp.zeros((256, CHUNK), jnp.int32)
    for r in range(1, 8):
        low = jnp.where(query_pos >= starts[r], starts[r], low)
    for part in range(3):
        key_pos = (c - 8) * 256 + part * CHUNK + lax.broadcasted_iota(jnp.int32, (256, CHUNK), 1)
        seen = (key_pos >= low) & (key_pos <= query_pos)
        bias[:, part * CHUNK:(part + 1) * CHUNK] = jnp.where(seen, 0.0, NEG)

    loads[4].wait()
    for owner in range(4):
        for pair in range(8):
            lanes = slice((owner * 8 + pair) * 128, (owner * 8 + pair + 1) * 128)
            value = jnp.concatenate([dqr[s, :, lanes].astype(F32) for s in range(3)], axis=0)
            for odd in range(2):
                flip[0, pl.ds(owner * 384 + pair * 2 + odd, 24, stride=16), :] = half_lanes(value, odd)
    for owner in range(4):
        qrope[owner] = flip[0, owner * 384:(owner + 1) * 384].reshape(24, 16, 128).astype(BF)

    loads[5].wait()
    loads[6].wait()
    for j in range(5):
        flip[j % 4, 0:128] = jnp.zeros((128, 128), F32)
        for s in range(3):
            if j < 4:
                value = nl[s, :, j * 128:(j + 1) * 128].astype(F32)
            else:
                value = nr[s].astype(F32)
                value = jnp.concatenate([value, value], axis=1)
            flip[j % 4, pl.ds(s, 8, stride=16), :] = value
        fresh[:, :, j * 128:(j + 1) * 128] = flip[j % 4, 0:128].reshape(8, 16, 128).astype(BF)

    loads[7].wait()
    loads[8].wait()
    old_rope = cr_st[...]
    pool[:, :, DL:] = jnp.concatenate([old_rope, old_rope], axis=2)

    loads[2].wait()
    loads[3].wait()
    for copy in z_copies:
        copy.wait_recv()

    def absorb(h, carry):
        lanes = pl.ds(pl.multiple_of(h * 128, 128), 128)
        value = jnp.concatenate(
            [qx[d, s, :, lanes].astype(F32) for d in range(4) for s in range(3)], axis=0)
        value = nn(value.astype(BF), upk[h])
        for j in range(4):
            flip[j, pl.ds(h, 96, stride=16), :] = value[:, j * 128:(j + 1) * 128]
        return carry

    lax.fori_loop(0, 16, absorb, 0)

    def spread(d, carry):
        for s in range(3):
            for i in range(8):
                base = pl.ds(pl.multiple_of((d * 24 + s * 8 + i) * 16, 16), 16)
                value = jnp.concatenate([flip[j, base, :] for j in range(4)], axis=1)
                qsend[d, (i // 2) * 6 + s * 2 + i % 2] = value.astype(BF)
        return carry

    lax.fori_loop(0, 4, spread, 0)

    q_copies = []
    for g in range(4):
        for d in (1, 2, 3):
            part = pl.ds(g * 6, 6)
            copy = remote(qsend.at[zp[d], part], qrecv.at[z, part],
                          q_send.at[d, g], q_recv.at[d, g], (zp[d], c))
            copy.start()
            q_copies.append(copy)
    q_own = pltpu.make_async_copy(qsend.at[z], qrecv.at[z], q_send.at[0, 0])
    q_own.start()

    got("a", -1)
    got("a", 1)
    push(("a2", 0), -1, 0, 1, 0, 0)
    push(("a2", 1), 1, 0, -1, 0, 1)
    for da in (-1, 1):
        push(("b", da, -1), da, 0, 0, 1)
        push(("b", da, 1), da, 0, 0, -1)
        share(da, 0)
    q_own.wait()

    row_step = lax.rem(lax.div(lax.broadcasted_iota(jnp.int32, (192, 16), 0), 16), 3)
    fresh_col = lax.broadcasted_iota(jnp.int32, (192, 16), 1)
    fresh_seen = (fresh_col <= row_step) & (fresh_col < 3)

    def attend(query, keys, used, recent):
        new = jnp.where(fresh_seen, nt(query, recent) * SCALE, NEG)
        scores = []
        top = jnp.max(new, axis=1, keepdims=True)
        for k in range(4):
            part = nt(query, keys(k)) * SCALE
            place = k * 512 + lax.broadcasted_iota(jnp.int32, (1, 512), 1)
            part = jnp.where(place < used, part, NEG)
            top = jnp.maximum(top, jnp.max(part, axis=1, keepdims=True))
            scores.append(part)
        new = jnp.exp2(new - top)
        total = jnp.sum(new, axis=1, keepdims=True)
        out = nn(new.astype(BF), recent[:, :DL])
        for k in range(4):
            part = jnp.exp2(scores[k] - top)
            total = total + jnp.sum(part, axis=1, keepdims=True)
            out = out + nn(part.astype(BF), keys(k)[:, :DL])
        return (out / total).astype(BF)

    def query_of(place, row):
        heads = [qrecv[o, place + 2 * s] for o in range(4) for s in range(3)]
        turns = [qrope[o, s * 8 + row] for o in range(4) for s in range(3)]
        return jnp.concatenate(
            [jnp.concatenate(heads, axis=0), jnp.concatenate(turns, axis=0)], axis=1)

    def decode_group(g):
        for e in range(2):
            row = 2 * g + e
            slot = row_slot[0, row]

            def keys(k):
                found = []
                for r in range(8):
                    page = jnp.minimum(pages[slot, k * 8 + r], 63)
                    found.append(pool[page])
                return jnp.concatenate(found, axis=0)

            out = attend(query_of(6 * g + e, row), keys, counts[slot], fresh[row])
            for o in range(4):
                for s in range(3):
                    obuf[o, 6 * g + 2 * s + e] = out[(o * 3 + s) * 16:(o * 3 + s + 1) * 16]

    o_copies = []

    def send_out(first, count, g):
        part = pl.ds(first, count)
        for d in (1, 2, 3):
            copy = remote(obuf.at[zp[d], part], orecv.at[z, part],
                          o_send.at[d, g], o_recv.at[d, g], (zp[d], c))
            copy.start()
            o_copies.append(copy)

    for g in range(4):
        for d in range(3):
            q_copies[g * 3 + d].wait_recv()
        decode_group(g)
        send_out(6 * g, 6, g)
        if g == 0:
            got("a2", 0)
            got("a2", 1)
            push(("b", 2, -1), 2, 0, 0, 1)
            push(("b", 2, 1), 2, 0, 0, -1)
            share(2, 0)
        if g == 1:
            for da in (0, -1, 1):
                got("b", da, -1)
                got("b", da, 1)
                push(("b2", da, 0), da, -1, 0, 1, 0)
                push(("b2", da, 1), da, 1, 0, -1, 1)
                share(da, -1)
                share(da, 1)
        if g == 2:
            got("b", 2, -1)
            got("b", 2, 1)
            push(("b2", 2, 0), 2, -1, 0, 1, 0)
            push(("b2", 2, 1), 2, 1, 0, -1, 1)
            share(2, -1)
            share(2, 1)
            for da in (0, -1, 1):
                got("b2", da, 0)
                got("b2", da, 1)
                share(da, 2)
        if g == 3:
            got("b2", 2, 0)
            got("b2", 2, 1)
            share(2, 2)
    for da in (0, -1, 1, 2):
        for db in (0, -1, 1, 2):
            got("s", da, db)

    device = z * 32 + c
    is_host = jnp.int32(0)
    arrival = jnp.int32(0)
    for r in range(8):
        hit = (hosts[r] == device).astype(jnp.int32)
        is_host = is_host + hit
        arrival = arrival + hit * lax.div(starts[r], PAGE)
    host_row = jnp.int32(0)
    for i in range(8):
        host_row = host_row + (row_slot[0, i] == 0).astype(jnp.int32) * i
    host_row = jnp.minimum(host_row, 7)

    def hosted_keys(k):
        found = []
        for r in range(8):
            page = jnp.minimum(arrival + k * 8 + r, 127)
            found.append(allb[page])
        return jnp.concatenate(found, axis=0)

    host_place = 6 * lax.div(host_row, 2) + lax.rem(host_row, 2)
    out = attend(query_of(host_place, host_row), hosted_keys, counts[0], fresh[host_row])
    for o in range(4):
        for s in range(3):
            obuf[o, 24 + s] = out[(o * 3 + s) * 16:(o * 3 + s + 1) * 16]
    send_out(24, 3, 4)

    loads[9].wait()
    loads[10].wait()
    loads[11].wait()

    def prefill_pair(p, carry):
        keys_up = upk[pl.ds(2 * p, 2)].reshape(256, DL)
        values_up = jnp.concatenate([upv[2 * p], upv[2 * p + 1]], axis=1)
        plain = qn[:, pl.ds(pl.multiple_of(p * 256, 256), 256)]
        turn = qr[:, pl.ds(pl.multiple_of(p * 128, 128), 128)]
        queries = [
            jnp.concatenate([plain[:, e * 128:(e + 1) * 128], half_lanes(turn, e)], axis=1)
            for e in range(2)
        ]
        state = [None, None]
        for part in (2, 1, 0):
            blocks = [lax.rem(c - 8 + part * 3 + i + 32, 32) for i in range(3)]
            rows_here = jnp.concatenate(
                [allb[pl.ds(block * 4, 4)].reshape(256, KW) for block in blocks], axis=0)
            latent = rows_here[:, :DL]
            head_keys = nt(latent, keys_up).astype(BF)
            head_values = nn(latent, values_up).astype(BF)
            shut = bias[:, part * CHUNK:(part + 1) * CHUNK]
            for e in range(2):
                key = jnp.concatenate([head_keys[:, e * 128:(e + 1) * 128], rows_here[:, DL:]], axis=1)
                value = jnp.concatenate(
                    [head_values[:, e * 128:(e + 1) * 128], jnp.ones((CHUNK, 128), BF)], axis=1)
                score = nt(queries[e], key) * SCALE + shut
                top = jnp.max(score, axis=1, keepdims=True)
                if state[e] is None:
                    weight = jnp.exp2(score - top)
                    total = nn(weight.astype(BF), value)
                else:
                    top = jnp.maximum(state[e][0], top)
                    weight = jnp.exp2(score - top)
                    total = state[e][1] * jnp.exp2(state[e][0] - top) + nn(weight.astype(BF), value)
                state[e] = (top, total)
        for e in range(2):
            total = state[e][1]
            pout[:, pl.ds(pl.multiple_of(p * 256 + e * 128, 128), 128)] = (
                total[:, :128] / total[:, 128:]).astype(BF)
        return carry

    lax.fori_loop(0, 8, prefill_pair, 0)
    pout_copy = pltpu.make_async_copy(pout, pout_h, out_sem.at[0])
    pout_copy.start()

    o_own = pltpu.make_async_copy(obuf.at[z, pl.ds(0, 27)], orecv.at[z, pl.ds(0, 27)], o_send.at[0, 0])
    o_own.start()
    for d in range(4):
        orecv[d, 27:32] = jnp.zeros((5, 16, DL), BF)
    for copy in o_copies:
        copy.wait_recv()
    o_own.wait()

    def unspread(t, carry):
        for u in range(8):
            value = orecv[lax.div(t, 4), lax.rem(t, 4) * 8 + u].astype(F32)
            base = pl.ds(pl.multiple_of((t * 8 + u) * 16, 16), 16)
            for j in range(4):
                flip[j, base, :] = value[:, j * 128:(j + 1) * 128]
        return carry

    lax.fori_loop(0, 16, unspread, 0)

    def project(h, carry):
        value = jnp.concatenate([flip[j, pl.ds(h, 128, stride=16), :] for j in range(4)], axis=1)
        value = nn(value.astype(BF), upv[h]).astype(BF)
        for d in range(4):
            ysend[d, :, pl.ds(pl.multiple_of(h * 128, 128), 128)] = value[d * 32:(d + 1) * 32]
        return carry

    lax.fori_loop(0, 16, project, 0)
    y_copies = []
    for d in (1, 2, 3):
        copy = remote(ysend.at[zp[d]], yrecv.at[z], y_send.at[d], y_recv.at[d], (zp[d], c))
        copy.start()
        y_copies.append(copy)
    y_own = pltpu.make_async_copy(ysend.at[z], yrecv.at[z], y_send.at[0])
    y_own.start()
    y_own.wait()
    for copy in y_copies:
        copy.wait_recv()

    row = lax.broadcasted_iota(jnp.int32, (8, 32), 0)
    place = lax.broadcasted_iota(jnp.int32, (8, 32), 1)
    for s in range(3):
        source = jnp.where((row == host_row) & (is_host > 0), 24 + s, lax.div(row, 2) * 6 + s * 2 + lax.rem(row, 2))
        pick = (place == source).astype(F32).astype(BF)
        for d in range(4):
            dout[s, :, d * 2048:(d + 1) * 2048] = nn(pick, yrecv[d]).astype(BF)
    dout_copy = pltpu.make_async_copy(dout, dout_h, out_sem.at[1])
    dout_copy.start()

    for copy in z_copies + q_copies + o_copies + y_copies + list(gather.values()):
        copy.wait_send()
    pout_copy.wait()
    dout_copy.wait()


def on_device(
    pre_q_nope, pre_q_rope, pre_latent, pre_rope, up_keys, up_values, new_lengths, new_hosts,
    req_pages, req_len, row_request, cache_latent, cache_rope, dec_q_nope, dec_q_rope,
    new_latent, new_rope,
):
    dma = pltpu.SemaphoreType.DMA
    vmem = pltpu.VMEM
    return pl.pallas_call(
        kernel,
        out_shape=(
            jax.ShapeDtypeStruct((256, 2048), BF),
            jax.ShapeDtypeStruct((3, 8, 8192), BF),
        ),
        in_specs=[pl.BlockSpec(memory_space=pltpu.SMEM)] * 5 + [pl.BlockSpec(memory_space=pl.ANY)] * 12,
        out_specs=[pl.BlockSpec(memory_space=pl.ANY)] * 2,
        scratch_shapes=[
            vmem((128, PAGE, KW), BF),
            vmem((4, PAGE, DR), BF),
            vmem((64, PAGE, KW), BF),
            vmem((64, PAGE, DR), BF),
            vmem((16, DN, DL), BF),
            vmem((16, DL, DV), BF),
            vmem((256, 2048), BF),
            vmem((256, 1024), BF),
            vmem((256, 2048), BF),
            vmem((256, 2304), F32),
            vmem((4, 3, 8, 2048), BF),
            vmem((3, 8, 4096), BF),
            vmem((3, 8, DL), BF),
            vmem((3, 8, DR), BF),
            vmem((4, 2048, 128), F32),
            vmem((4, 24, 16, DL), BF),
            vmem((4, 24, 16, DL), BF),
            vmem((4, 24, 16, 128), BF),
            vmem((8, 16, KW), BF),
            vmem((4, 32, 16, DL), BF),
            vmem((4, 32, 16, DL), BF),
            vmem((4, 32, 2048), BF),
            vmem((4, 32, 2048), BF),
            vmem((3, 8, 8192), BF),
            dma((12,)),
            dma((4,)), dma((4,)),
            dma((4, 4)), dma((4, 4)),
            dma((4, 5)), dma((4, 5)),
            dma((4,)), dma((4,)),
            dma((36,)), dma((36,)),
            dma((2,)),
        ],
        compiler_params=pltpu.CompilerParams(
            collective_id=0, has_side_effects=True, vmem_limit_bytes=60 * 2**20),
        cost_estimate=pl.CostEstimate(flops=25 * 10**9, bytes_accessed=16 * 2**20, transcendentals=12 * 10**6),
    )(
        new_lengths, new_hosts, req_pages, req_len, row_request,
        pre_q_nope, pre_q_rope, pre_latent.reshape(4, PAGE, DL), pre_rope.reshape(4, PAGE, DR), up_keys, up_values,
        cache_latent.reshape(64, PAGE, DL), cache_rope.reshape(64, PAGE, DR), dec_q_nope, dec_q_rope, new_latent, new_rope,
    )


def solution(mesh):
    placed = (
        P("cp", "dp"),
        P("cp", "dp"),
        P("cp", None),
        P("cp", None),
        P("dp", None, None),
        P("dp", None, None),
        P(),
        P(),
        P(("dp", "cp"), None),
        P(("dp", "cp")),
        P(("dp", "cp"), None),
        P(("dp", "cp"), None),
        P(("dp", "cp"), None),
        P(None, ("dp", "cp"), None),
        P(None, ("dp", "cp"), None),
        P(None, ("dp", "cp"), None),
        P(None, ("dp", "cp"), None),
    )
    return jax.shard_map(
        on_device,
        mesh=mesh,
        in_specs=placed,
        out_specs=(P("cp", "dp"), P(None, ("dp", "cp"), None)),
        check_vma=False,
    )
```

```python
import jax
import jax.numpy as jnp
from jax import lax
from jax.experimental import pallas as pl
from jax.experimental.pallas import tpu as pltpu
from jax.sharding import PartitionSpec as P

DN, DR, DL, DV, PAGE = 128, 64, 512, 128, 64
F32, BF = jnp.float32, jnp.bfloat16
SCALE = (DN + DR) ** -0.5 * 1.4426950408889634
NEG = -1e30
KW = DL + 2 * DR
CHUNK = 768
MESH = pl.DeviceIdType.MESH


def nt(a, b):
    return lax.dot_general(a, b, (((1,), (1,)), ((), ())), preferred_element_type=F32)


def nn(a, b):
    return lax.dot_general(a, b, (((1,), (0,)), ((), ())), preferred_element_type=F32)


def half_lanes(pair, odd):
    lane = lax.broadcasted_iota(jnp.int32, pair.shape, 1)
    return jnp.where((lane >= DR) if odd else (lane < DR), pair, jnp.zeros_like(pair))


def kernel(
    lengths, hosts, pages, counts, row_slot,
    qn_h, qr_h, lat_h, rope_h, upk_h, upv_h, cl_h, cr_h, dq_h, dqr_h, nl_h, nr_h,
    pout_h, dout_h,
    allb, rope_st, pool, cr_st, upk, upv, qn, qr, pout, bias,
    qx, dqr, nl, nr, tops, totals, flip, qsend, qrecv, qrope, fresh, obuf, orecv, ysend, yrecv, dout,
    load_sem, z_send, z_recv, q_send, q_recv, o_send, o_recv, y_send, y_recv,
    a_send, a_recv, near_send, near_recv, out_sem,
):
    z = lax.axis_index("dp")
    c = lax.axis_index("cp")
    core = lax.rem(c, 2)
    chip = lax.div(c, 2)
    cx, cy = lax.rem(chip, 4), lax.div(chip, 4)
    a = cx + core * (cy - cx)
    b = cy + core * (cx - cy)

    def at(da, db):
        pa, pb = lax.rem(a + da + 4, 4), lax.rem(b + db + 4, 4)
        return 2 * (pa * (1 + 3 * core) + pb * (4 - 3 * core)) + core

    sibling = c + 1 - 2 * core
    zp = [lax.rem(z + d, 4) for d in range(4)]

    loads = [
        (lat_h, allb.at[pl.ds(4 * c, 4), :, pl.ds(0, DL)]),
        (rope_h, rope_st),
        (dq_h.at[:, :, pl.ds(pl.multiple_of(z * 2048, 2048), 2048)], qx.at[z]),
        (upk_h, upk),
        (dqr_h, dqr),
        (nl_h, nl),
        (nr_h, nr),
        (cl_h, pool.at[:, :, pl.ds(0, DL)]),
        (cr_h, cr_st),
        (qn_h, qn),
        (qr_h, qr),
        (upv_h, upv),
    ]
    loads = [pltpu.make_async_copy(s, d, load_sem.at[i]) for i, (s, d) in enumerate(loads)]
    for one in loads:
        one.start()

    barrier = pltpu.get_barrier_semaphore()
    peers = [(z, at(1, 0)), (z, at(-1, 0)), (z, at(0, 1)), (z, at(0, -1)), (z, sibling)]
    after, before = lax.rem(c + 2, 32), lax.rem(c + 30, 32)
    peers += [(zp[d], c) for d in (1, 2, 3)] + [(z, after), (z, before)]
    for peer in peers:
        pl.semaphore_signal(barrier, inc=1, device_id=peer, device_id_type=MESH)
    pl.semaphore_wait(barrier, len(peers))

    def remote(src, dst, send, recv, peer):
        return pltpu.make_async_remote_copy(
            src_ref=src, dst_ref=dst, send_sem=send, recv_sem=recv,
            device_id=peer, device_id_type=MESH)

    z_copies = []
    for d in (1, 2, 3):
        cols = pl.ds(pl.multiple_of(zp[d] * 2048, 2048), 2048)
        z_copies.append(remote(dq_h.at[:, :, cols], qx.at[z], z_send.at[d], z_recv.at[d], (zp[d], c)))
        z_copies[-1].start()

    loads[0].wait()
    loads[1].wait()
    own_rope = rope_st[...].astype(F32)
    own_rope = jnp.concatenate([own_rope, own_rope], axis=0).T
    allb[pl.ds(4 * c, 4), :, DL:] = own_rope.reshape(4, PAGE, 128).astype(BF)

    def rows(block, half=None):
        if half is None:
            return allb.at[pl.ds(block * 4, 4)]
        return allb.at[pl.ds(block * 4 + half * 2, 2)]

    near = [
        remote(rows(c), rows(32), near_send.at[0], near_recv.at[0], (z, after)),
        remote(rows(c), rows(33), near_send.at[1], near_recv.at[1], (z, sibling)),
        remote(rows(32), rows(34), near_send.at[2], near_recv.at[2], (z, sibling)),
    ]
    near[0].start()
    near[1].start()

    gather = {}
    slots = [0]

    def push(key, da, db, pa, pb, half=None):
        i = slots[0]
        slots[0] += 1
        ref = rows(at(da, db), half)
        copy = remote(ref, ref, a_send.at[i], a_recv.at[i], (z, at(pa, pb)))
        copy.start()
        gather[key] = copy

    def share(da, db):
        i = slots[0]
        slots[0] += 1
        ref = rows(at(da, db))
        copy = remote(ref, ref, a_send.at[i], a_recv.at[i], (z, sibling))
        copy.start()
        gather["s", da, db] = copy

    def got(*key):
        gather[key].wait_recv()

    push(("a", -1), 0, 0, 1, 0)
    push(("a", 1), 0, 0, -1, 0)
    push(("b", 0, -1), 0, 0, 0, 1)
    push(("b", 0, 1), 0, 0, 0, -1)
    share(0, 0)

    starts = [jnp.int32(0)]
    for r in range(7):
        starts.append(starts[-1] + lengths[r] * PAGE)
    query_pos = c * 256 + lax.broadcasted_iota(jnp.int32, (256, CHUNK), 0)
    low = jnp.zeros((256, CHUNK), jnp.int32)
    for r in range(1, 8):
        low = jnp.where(query_pos >= starts[r], starts[r], low)
    for part in range(3):
        key_pos = (c - 8) * 256 + part * CHUNK + lax.broadcasted_iota(jnp.int32, (256, CHUNK), 1)
        seen = (key_pos >= low) & (key_pos <= query_pos)
        bias[:, part * CHUNK:(part + 1) * CHUNK] = jnp.where(seen, 0.0, NEG)

    loads[4].wait()
    for owner in range(4):
        for pair in range(8):
            lanes = slice((owner * 8 + pair) * 128, (owner * 8 + pair + 1) * 128)
            value = jnp.concatenate([dqr[s, :, lanes].astype(F32) for s in range(3)], axis=0)
            for odd in range(2):
                flip[0, pl.ds(owner * 384 + pair * 2 + odd, 24, stride=16), :] = half_lanes(value, odd)
    for owner in range(4):
        qrope[owner] = flip[0, owner * 384:(owner + 1) * 384].reshape(24, 16, 128).astype(BF)

    loads[5].wait()
    loads[6].wait()
    for j in range(5):
        flip[j % 4, 0:128] = jnp.zeros((128, 128), F32)
        for s in range(3):
            if j < 4:
                value = nl[s, :, j * 128:(j + 1) * 128].astype(F32)
            else:
                value = nr[s].astype(F32)
                value = jnp.concatenate([value, value], axis=1)
            flip[j % 4, pl.ds(s, 8, stride=16), :] = value
        fresh[:, :, j * 128:(j + 1) * 128] = flip[j % 4, 0:128].reshape(8, 16, 128).astype(BF)

    loads[7].wait()
    loads[8].wait()
    for i in range(8):
        old_rope = cr_st[:, i * 512:(i + 1) * 512].astype(F32)
        old_rope = jnp.concatenate([old_rope, old_rope], axis=0).T
        pool[i * 8:(i + 1) * 8, :, DL:] = old_rope.reshape(8, PAGE, 128).astype(BF)

    near[0].wait_recv()
    near[2].start()

    loads[2].wait()
    loads[3].wait()
    for copy in z_copies:
        copy.wait_recv()

    def absorb(h, carry):
        lanes = pl.ds(pl.multiple_of(h * 128, 128), 128)
        value = jnp.concatenate(
            [qx[d, s, :, lanes].astype(F32) for d in range(4) for s in range(3)], axis=0)
        value = nn(value.astype(BF), upk[h])
        for j in range(4):
            flip[j, pl.ds(h, 96, stride=16), :] = value[:, j * 128:(j + 1) * 128]
        return carry

    lax.fori_loop(0, 16, absorb, 0, unroll=4)

    def spread(d, carry):
        for s in range(3):
            for i in range(8):
                base = pl.ds(pl.multiple_of((d * 24 + s * 8 + i) * 16, 16), 16)
                value = jnp.concatenate([flip[j, base, :] for j in range(4)], axis=1)
                qsend[d, (i // 2) * 6 + s * 2 + i % 2] = value.astype(BF)
        return carry

    lax.fori_loop(0, 4, spread, 0)

    q_copies = []
    for g in range(4):
        for d in (1, 2, 3):
            part = pl.ds(g * 6, 6)
            copy = remote(qsend.at[zp[d], part], qrecv.at[z, part],
                          q_send.at[d, g], q_recv.at[d, g], (zp[d], c))
            copy.start()
            q_copies.append(copy)
    q_own = pltpu.make_async_copy(qsend.at[z], qrecv.at[z], q_send.at[0, 0])
    q_own.start()

    got("a", -1)
    got("a", 1)
    push(("a2", 0), -1, 0, 1, 0, 0)
    push(("a2", 1), 1, 0, -1, 0, 1)
    for da in (-1, 1):
        push(("b", da, -1), da, 0, 0, 1)
        push(("b", da, 1), da, 0, 0, -1)
        share(da, 0)
    q_own.wait()

    def prefill_part(p, part, state):
        keys_up = upk[pl.ds(2 * p, 2)].reshape(256, DL)
        values_up = jnp.concatenate([upv[2 * p], upv[2 * p + 1]], axis=1)
        plain = qn[:, pl.ds(pl.multiple_of(p * 256, 256), 256)]
        turn = qr[:, pl.ds(pl.multiple_of(p * 128, 128), 128)]
        if part == 2:
            blocks = [32, 34 - core, c]
        else:
            blocks = [lax.rem(c - 8 + part * 3 + i + 32, 32) for i in range(3)]
        rows_here = jnp.concatenate(
            [allb[pl.ds(block * 4, 4)].reshape(256, KW) for block in blocks], axis=0)
        latent = rows_here[:, :DL]
        head_keys = nt(latent, keys_up).astype(BF)
        head_values = nn(latent, values_up).astype(BF)
        shut = bias[:, part * CHUNK:(part + 1) * CHUNK]
        following = []
        for e in range(2):
            query = jnp.concatenate([plain[:, e * 128:(e + 1) * 128], half_lanes(turn, e)], axis=1)
            key = jnp.concatenate([head_keys[:, e * 128:(e + 1) * 128], rows_here[:, DL:]], axis=1)
            value = jnp.concatenate(
                [head_values[:, e * 128:(e + 1) * 128], jnp.ones((CHUNK, 128), BF)], axis=1)
            score = nt(query, key) * SCALE + shut
            top = jnp.max(score, axis=1, keepdims=True)
            if state is None:
                weight = jnp.exp2(score - top)
                total = nn(weight.astype(BF), value)
            else:
                old_top, old_total = state[e]
                top = jnp.maximum(old_top, top)
                weight = jnp.exp2(score - top)
                total = old_total * jnp.exp2(old_top - top) + nn(weight.astype(BF), value)
            following.append((top, total))
        return following

    def prefill_near(p, carry):
        for e, (top, total) in enumerate(prefill_part(p, 2, None)):
            lane = lax.broadcasted_iota(jnp.int32, (256, 128), 1)
            tops[2 * p + e] = jnp.where(lane < 64, top, total[:, 128:])
            totals[2 * p + e] = total[:, :128]
        return carry

    def prefill_far(p, carry):
        state = []
        for e in range(2):
            known = tops[2 * p + e]
            summed = jnp.broadcast_to(known[:, 64:65], (256, 128))
            state.append((known[:, :1], jnp.concatenate([totals[2 * p + e], summed], axis=1)))
        for part in (1, 0):
            state = prefill_part(p, part, state)
        for e in range(2):
            total = state[e][1]
            pout[:, pl.ds(pl.multiple_of(p * 256 + e * 128, 128), 128)] = (
                total[:, :128] / total[:, 128:]).astype(BF)
        return carry

    near[1].wait_recv()
    near[2].wait_recv()
    loads[9].wait()
    loads[10].wait()
    loads[11].wait()
    lax.fori_loop(0, 4, prefill_near, 0, unroll=2)
    got("a2", 0)
    got("a2", 1)
    push(("b", 2, -1), 2, 0, 0, 1)
    push(("b", 2, 1), 2, 0, 0, -1)
    share(2, 0)
    got("b", 0, -1)
    got("b", 0, 1)
    push(("b2", 0, 0), 0, -1, 0, 1, 0)
    push(("b2", 0, 1), 0, 1, 0, -1, 1)
    share(0, -1)
    share(0, 1)
    lax.fori_loop(4, 8, prefill_near, 0, unroll=2)

    row_step = lax.rem(lax.div(lax.broadcasted_iota(jnp.int32, (192, 16), 0), 16), 3)
    fresh_col = lax.broadcasted_iota(jnp.int32, (192, 16), 1)
    fresh_seen = (fresh_col <= row_step) & (fresh_col < 3)

    def attend(queries, keys, used, recent):
        count = len(queries)
        new, scores, top = [], [[] for _ in range(count)], []
        for e in range(count):
            new.append(jnp.where(fresh_seen, nt(queries[e], recent[e]) * SCALE, NEG))
            top.append(jnp.max(new[e], axis=1, keepdims=True))
        for k in range(4):
            place = k * 512 + lax.broadcasted_iota(jnp.int32, (1, 512), 1)
            for e in range(count):
                part = nt(queries[e], keys(e, k)) * SCALE
                part = jnp.where(place < used[e], part, NEG)
                top[e] = jnp.maximum(top[e], jnp.max(part, axis=1, keepdims=True))
                scores[e].append(part)
        total, out = [], []
        for e in range(count):
            fresh_weight = jnp.exp2(new[e] - top[e])
            total.append(jnp.sum(fresh_weight, axis=1, keepdims=True))
            out.append(nn(fresh_weight.astype(BF), recent[e][:, :DL]))
        for k in range(4):
            for e in range(count):
                part = jnp.exp2(scores[e][k] - top[e])
                total[e] = total[e] + jnp.sum(part, axis=1, keepdims=True)
                out[e] = out[e] + nn(part.astype(BF), keys(e, k)[:, :DL])
        return [(out[e] / total[e]).astype(BF) for e in range(count)]

    def query_of(place, row):
        heads = [qrecv[o, place + 2 * s] for o in range(4) for s in range(3)]
        turns = [qrope[o, s * 8 + row] for o in range(4) for s in range(3)]
        return jnp.concatenate(
            [jnp.concatenate(heads, axis=0), jnp.concatenate(turns, axis=0)], axis=1)

    def decode_group(g):
        slots_here = [row_slot[0, 2 * g + e] for e in range(2)]

        def keys(e, k):
            found = []
            for r in range(8):
                page = jnp.minimum(pages[slots_here[e], k * 8 + r], 63)
                found.append(pool[page])
            return jnp.concatenate(found, axis=0)

        outs = attend(
            [query_of(6 * g + e, 2 * g + e) for e in range(2)], keys,
            [counts[slot] for slot in slots_here], [fresh[2 * g + e] for e in range(2)])
        for e in range(2):
            for o in range(4):
                for s in range(3):
                    obuf[o, 6 * g + 2 * s + e] = outs[e][(o * 3 + s) * 16:(o * 3 + s + 1) * 16]

    o_copies = []

    def send_out(first, count, g):
        part = pl.ds(first, count)
        for d in (1, 2, 3):
            copy = remote(obuf.at[zp[d], part], orecv.at[z, part],
                          o_send.at[d, g], o_recv.at[d, g], (zp[d], c))
            copy.start()
            o_copies.append(copy)

    for g in range(4):
        for d in range(3):
            q_copies[g * 3 + d].wait_recv()
        decode_group(g)
        send_out(6 * g, 6, g)
        if g == 0:
            for da in (-1, 1):
                got("b", da, -1)
                got("b", da, 1)
                push(("b2", da, 0), da, -1, 0, 1, 0)
                push(("b2", da, 1), da, 1, 0, -1, 1)
                share(da, -1)
                share(da, 1)
        if g == 1:
            got("b", 2, -1)
            got("b", 2, 1)
            push(("b2", 2, 0), 2, -1, 0, 1, 0)
            push(("b2", 2, 1), 2, 1, 0, -1, 1)
            share(2, -1)
            share(2, 1)
            got("b2", 0, 0)
            got("b2", 0, 1)
            share(0, 2)
        if g == 2:
            for da in (-1, 1):
                got("b2", da, 0)
                got("b2", da, 1)
                share(da, 2)
        if g == 3:
            got("b2", 2, 0)
            got("b2", 2, 1)
            share(2, 2)
    for da in (0, -1, 1, 2):
        for db in (0, -1, 1, 2):
            got("s", da, db)

    device = z * 32 + c
    is_host = jnp.int32(0)
    arrival = jnp.int32(0)
    for r in range(8):
        hit = (hosts[r] == device).astype(jnp.int32)
        is_host = is_host + hit
        arrival = arrival + hit * lax.div(starts[r], PAGE)
    host_row = jnp.int32(0)
    for i in range(8):
        host_row = host_row + (row_slot[0, i] == 0).astype(jnp.int32) * i
    host_row = jnp.minimum(host_row, 7)

    def hosted_keys(e, k):
        found = []
        for r in range(8):
            page = jnp.minimum(arrival + k * 8 + r, 127)
            found.append(allb[page])
        return jnp.concatenate(found, axis=0)

    host_place = 6 * lax.div(host_row, 2) + lax.rem(host_row, 2)
    out = attend([query_of(host_place, host_row)], hosted_keys, [counts[0]], [fresh[host_row]])[0]
    for o in range(4):
        for s in range(3):
            obuf[o, 24 + s] = out[(o * 3 + s) * 16:(o * 3 + s + 1) * 16]
    send_out(24, 3, 4)

    early = 6
    lax.fori_loop(0, early, prefill_far, 0, unroll=2)
    pout_copies = [
        pltpu.make_async_copy(pout.at[:, pl.ds(0, early * 256)], pout_h.at[:, pl.ds(0, early * 256)], out_sem.at[0])]
    pout_copies[0].start()

    o_own = pltpu.make_async_copy(obuf.at[z, pl.ds(0, 27)], orecv.at[z, pl.ds(0, 27)], o_send.at[0, 0])
    o_own.start()
    for d in range(4):
        orecv[d, 27:32] = jnp.zeros((5, 16, DL), BF)
    for copy in o_copies:
        copy.wait_recv()
    o_own.wait()

    def unspread(t, carry):
        for u in range(8):
            value = orecv[lax.div(t, 4), lax.rem(t, 4) * 8 + u].astype(F32)
            base = pl.ds(pl.multiple_of((t * 8 + u) * 16, 16), 16)
            for j in range(4):
                flip[j, base, :] = value[:, j * 128:(j + 1) * 128]
        return carry

    lax.fori_loop(0, 16, unspread, 0)

    def project(h, carry):
        value = jnp.concatenate([flip[j, pl.ds(h, 128, stride=16), :] for j in range(4)], axis=1)
        value = nn(value.astype(BF), upv[h]).astype(BF)
        for d in range(4):
            ysend[d, :, pl.ds(pl.multiple_of(h * 128, 128), 128)] = value[d * 32:(d + 1) * 32]
        return carry

    lax.fori_loop(0, 16, project, 0, unroll=4)
    y_copies = []
    for d in (1, 2, 3):
        copy = remote(ysend.at[zp[d]], yrecv.at[z], y_send.at[d], y_recv.at[d], (zp[d], c))
        copy.start()
        y_copies.append(copy)
    y_own = pltpu.make_async_copy(ysend.at[z], yrecv.at[z], y_send.at[0])
    y_own.start()

    lax.fori_loop(early, 8, prefill_far, 0, unroll=2)
    late = pl.ds(early * 256, 2048 - early * 256)
    pout_copies.append(pltpu.make_async_copy(pout.at[:, late], pout_h.at[:, late], out_sem.at[2]))
    pout_copies[1].start()
    y_own.wait()
    for copy in y_copies:
        copy.wait_recv()

    row = lax.broadcasted_iota(jnp.int32, (8, 32), 0)
    place = lax.broadcasted_iota(jnp.int32, (8, 32), 1)
    for s in range(3):
        source = jnp.where((row == host_row) & (is_host > 0), 24 + s, lax.div(row, 2) * 6 + s * 2 + lax.rem(row, 2))
        pick = (place == source).astype(F32).astype(BF)
        for d in range(4):
            dout[s, :, d * 2048:(d + 1) * 2048] = nn(pick, yrecv[d]).astype(BF)
    dout_copy = pltpu.make_async_copy(dout, dout_h, out_sem.at[1])
    dout_copy.start()

    for copy in z_copies + q_copies + o_copies + y_copies + list(gather.values()):
        copy.wait_send()
    for copy in near:
        copy.wait_send()
    for copy in pout_copies:
        copy.wait()
    dout_copy.wait()


def on_device(
    pre_q_nope, pre_q_rope, pre_latent, pre_rope, up_keys, up_values, new_lengths, new_hosts,
    req_pages, req_len, row_request, cache_latent, cache_rope, dec_q_nope, dec_q_rope,
    new_latent, new_rope,
):
    dma = pltpu.SemaphoreType.DMA
    vmem = pltpu.VMEM
    return pl.pallas_call(
        kernel,
        out_shape=(
            jax.ShapeDtypeStruct((256, 2048), BF),
            jax.ShapeDtypeStruct((3, 8, 8192), BF),
        ),
        in_specs=[pl.BlockSpec(memory_space=pltpu.SMEM)] * 5 + [pl.BlockSpec(memory_space=pl.ANY)] * 12,
        out_specs=[pl.BlockSpec(memory_space=pl.ANY)] * 2,
        scratch_shapes=[
            vmem((140, PAGE, KW), BF),
            vmem((DR, 256), BF),
            vmem((64, PAGE, KW), BF),
            vmem((DR, 4096), BF),
            vmem((16, DN, DL), BF),
            vmem((16, DL, DV), BF),
            vmem((256, 2048), BF),
            vmem((256, 1024), BF),
            vmem((256, 2048), BF),
            vmem((256, 2304), F32),
            vmem((4, 3, 8, 2048), BF),
            vmem((3, 8, 4096), BF),
            vmem((3, 8, DL), BF),
            vmem((3, 8, DR), BF),
            vmem((16, 256, 128), F32),
            vmem((16, 256, 128), F32),
            vmem((4, 2048, 128), F32),
            vmem((4, 24, 16, DL), BF),
            vmem((4, 24, 16, DL), BF),
            vmem((4, 24, 16, 128), BF),
            vmem((8, 16, KW), BF),
            vmem((4, 32, 16, DL), BF),
            vmem((4, 32, 16, DL), BF),
            vmem((4, 32, 2048), BF),
            vmem((4, 32, 2048), BF),
            vmem((3, 8, 8192), BF),
            dma((12,)),
            dma((4,)), dma((4,)),
            dma((4, 4)), dma((4, 4)),
            dma((4, 5)), dma((4, 5)),
            dma((4,)), dma((4,)),
            dma((36,)), dma((36,)),
            dma((3,)), dma((3,)),
            dma((3,)),
        ],
        compiler_params=pltpu.CompilerParams(
            collective_id=0, has_side_effects=True, vmem_limit_bytes=60 * 2**20),
        cost_estimate=pl.CostEstimate(flops=25 * 10**9, bytes_accessed=16 * 2**20, transcendentals=12 * 10**6),
    )(
        new_lengths, new_hosts, req_pages, req_len, row_request,
        pre_q_nope, pre_q_rope, pre_latent.reshape(4, PAGE, DL), pre_rope.T, up_keys, up_values,
        cache_latent.reshape(64, PAGE, DL), cache_rope.T, dec_q_nope, dec_q_rope, new_latent, new_rope,
    )


def solution(mesh):
    placed = (
        P("cp", "dp"),
        P("cp", "dp"),
        P("cp", None),
        P("cp", None),
        P("dp", None, None),
        P("dp", None, None),
        P(),
        P(),
        P(("dp", "cp"), None),
        P(("dp", "cp")),
        P(("dp", "cp"), None),
        P(("dp", "cp"), None),
        P(("dp", "cp"), None),
        P(None, ("dp", "cp"), None),
        P(None, ("dp", "cp"), None),
        P(None, ("dp", "cp"), None),
        P(None, ("dp", "cp"), None),
    )
    return jax.shard_map(
        on_device,
        mesh=mesh,
        in_specs=placed,
        out_specs=(P("cp", "dp"), P(None, ("dp", "cp"), None)),
        check_vma=False,
    )
```

```python
import jax
import jax.numpy as jnp
from jax import lax
from jax.experimental import pallas as pl
from jax.experimental.pallas import tpu as pltpu
from jax.sharding import PartitionSpec as P

DN, DR, DL, DV, PAGE = 128, 64, 512, 128, 64
F32, BF = jnp.float32, jnp.bfloat16
SCALE = (DN + DR) ** -0.5 * 1.4426950408889634
NEG = -1e30
KW = DL + 2 * DR
CHUNK = 768
MESH = pl.DeviceIdType.MESH


def nt(a, b):
    return lax.dot_general(a, b, (((1,), (1,)), ((), ())), preferred_element_type=F32)


def nn(a, b):
    return lax.dot_general(a, b, (((1,), (0,)), ((), ())), preferred_element_type=F32)


def half_lanes(pair, odd):
    lane = lax.broadcasted_iota(jnp.int32, pair.shape, 1)
    return jnp.where((lane >= DR) if odd else (lane < DR), pair, jnp.zeros_like(pair))


def kernel(
    lengths, hosts, pages, counts, row_slot,
    qn_h, qr_h, lat_h, rope_h, upk_h, upv_h, cl_h, cr_h, dq_h, dqr_h, nl_h, nr_h,
    pout_h, dout_h,
    allb, rope_st, pool, cr_st, upk, upv, qn, qr, pout, bias,
    qx, dqr, nl, nr, tops, totals, flip, qsend, qrecv, qrope, fresh, obuf, orecv, ysend, yrecv, dout,
    load_sem, z_send, z_recv, q_send, q_recv, o_send, o_recv, y_send, y_recv,
    a_send, a_recv, near_send, near_recv, out_sem,
):
    z = lax.axis_index("dp")
    c = lax.axis_index("cp")
    core = lax.rem(c, 2)
    chip = lax.div(c, 2)
    cx, cy = lax.rem(chip, 4), lax.div(chip, 4)
    a = cx + core * (cy - cx)
    b = cy + core * (cx - cy)

    def at(da, db):
        pa, pb = lax.rem(a + da + 4, 4), lax.rem(b + db + 4, 4)
        return 2 * (pa * (1 + 3 * core) + pb * (4 - 3 * core)) + core

    sibling = c + 1 - 2 * core
    zp = [lax.rem(z + d, 4) for d in range(4)]

    loads = [
        (lat_h, allb.at[pl.ds(4 * c, 4), :, pl.ds(0, DL)]),
        (rope_h, rope_st),
        (dq_h.at[:, :, pl.ds(pl.multiple_of(z * 2048, 2048), 2048)], qx.at[z]),
        (upk_h, upk),
        (dqr_h, dqr),
        (nl_h, nl),
        (nr_h, nr),
        (cl_h, pool.at[:, :, pl.ds(0, DL)]),
        (cr_h, cr_st),
        (qn_h, qn),
        (qr_h, qr),
        (upv_h, upv),
    ]
    loads = [pltpu.make_async_copy(s, d, load_sem.at[i]) for i, (s, d) in enumerate(loads)]
    for one in loads[:4]:
        one.start()

    barrier = pltpu.get_barrier_semaphore()
    peers = [(z, at(1, 0)), (z, at(-1, 0)), (z, at(0, 1)), (z, at(0, -1)), (z, sibling)]
    after, before = lax.rem(c + 2, 32), lax.rem(c + 30, 32)
    peers += [(zp[d], c) for d in (1, 2, 3)] + [(z, after), (z, before)]
    for peer in peers:
        pl.semaphore_signal(barrier, inc=1, device_id=peer, device_id_type=MESH)
    pl.semaphore_wait(barrier, len(peers))

    def remote(src, dst, send, recv, peer):
        return pltpu.make_async_remote_copy(
            src_ref=src, dst_ref=dst, send_sem=send, recv_sem=recv,
            device_id=peer, device_id_type=MESH)

    z_copies = []
    for d in (1, 2, 3):
        cols = pl.ds(pl.multiple_of(zp[d] * 2048, 2048), 2048)
        z_copies.append(remote(dq_h.at[:, :, cols], qx.at[z], z_send.at[d], z_recv.at[d], (zp[d], c)))
        z_copies[-1].start()

    loads[0].wait()
    loads[1].wait()
    own_rope = rope_st[...].astype(F32)
    own_rope = jnp.concatenate([own_rope, own_rope], axis=0).T
    allb[pl.ds(4 * c, 4), :, DL:] = own_rope.reshape(4, PAGE, 128).astype(BF)

    def rows(block, half=None):
        if half is None:
            return allb.at[pl.ds(block * 4, 4)]
        return allb.at[pl.ds(block * 4 + half * 2, 2)]

    jump = remote(rows(c), rows(32), near_send.at[0], near_recv.at[0], (z, after))
    jump_share = remote(rows(32), rows(33), near_send.at[1], near_recv.at[1], (z, sibling))

    @pl.when(cx == 3)
    def _():
        jump.start()

    gather = {}
    slots = [0]

    def push(key, da, db, pa, pb, half=None):
        i = slots[0]
        slots[0] += 1
        ref = rows(at(da, db), half)
        copy = remote(ref, ref, a_send.at[i], a_recv.at[i], (z, at(pa, pb)))
        copy.start()
        gather[key] = copy

    def share(da, db):
        i = slots[0]
        slots[0] += 1
        ref = rows(at(da, db))
        copy = remote(ref, ref, a_send.at[i], a_recv.at[i], (z, sibling))
        copy.start()
        gather["s", da, db] = copy

    def got(*key):
        gather[key].wait_recv()

    push(("a", -1), 0, 0, 1, 0)
    push(("a", 1), 0, 0, -1, 0)
    push(("b", 0, -1), 0, 0, 0, 1)
    push(("b", 0, 1), 0, 0, 0, -1)
    share(0, 0)
    for one in loads[4:]:
        one.start()

    starts = [jnp.int32(0)]
    for r in range(7):
        starts.append(starts[-1] + lengths[r] * PAGE)
    query_pos = c * 256 + lax.broadcasted_iota(jnp.int32, (256, CHUNK), 0)
    low = jnp.zeros((256, CHUNK), jnp.int32)
    for r in range(1, 8):
        low = jnp.where(query_pos >= starts[r], starts[r], low)
    for part in range(3):
        key_pos = (c - 8) * 256 + part * CHUNK + lax.broadcasted_iota(jnp.int32, (256, CHUNK), 1)
        seen = (key_pos >= low) & (key_pos <= query_pos)
        bias[:, part * CHUNK:(part + 1) * CHUNK] = jnp.where(seen, 0.0, NEG)

    loads[4].wait()
    for owner in range(4):
        for pair in range(8):
            lanes = slice((owner * 8 + pair) * 128, (owner * 8 + pair + 1) * 128)
            value = jnp.concatenate([dqr[s, :, lanes].astype(F32) for s in range(3)], axis=0)
            for odd in range(2):
                flip[0, pl.ds(owner * 384 + pair * 2 + odd, 24, stride=16), :] = half_lanes(value, odd)
    for owner in range(4):
        qrope[owner] = flip[0, owner * 384:(owner + 1) * 384].reshape(24, 16, 128).astype(BF)

    loads[5].wait()
    loads[6].wait()
    for j in range(5):
        flip[j % 4, 0:128] = jnp.zeros((128, 128), F32)
        for s in range(3):
            if j < 4:
                value = nl[s, :, j * 128:(j + 1) * 128].astype(F32)
            else:
                value = nr[s].astype(F32)
                value = jnp.concatenate([value, value], axis=1)
            flip[j % 4, pl.ds(s, 8, stride=16), :] = value
        fresh[:, :, j * 128:(j + 1) * 128] = flip[j % 4, 0:128].reshape(8, 16, 128).astype(BF)

    loads[7].wait()
    loads[8].wait()
    for i in range(8):
        old_rope = cr_st[:, i * 512:(i + 1) * 512].astype(F32)
        old_rope = jnp.concatenate([old_rope, old_rope], axis=0).T
        pool[i * 8:(i + 1) * 8, :, DL:] = old_rope.reshape(8, PAGE, 128).astype(BF)

    loads[2].wait()
    loads[3].wait()
    for copy in z_copies:
        copy.wait_recv()

    def absorb(h, carry):
        lanes = pl.ds(pl.multiple_of(h * 128, 128), 128)
        value = jnp.concatenate(
            [qx[d, s, :, lanes].astype(F32) for d in range(4) for s in range(3)], axis=0)
        value = nn(value.astype(BF), upk[h])
        for j in range(4):
            flip[j, pl.ds(h, 96, stride=16), :] = value[:, j * 128:(j + 1) * 128]
        return carry

    lax.fori_loop(0, 16, absorb, 0, unroll=4)

    def spread(d, carry):
        for s in range(3):
            for i in range(8):
                base = pl.ds(pl.multiple_of((d * 24 + s * 8 + i) * 16, 16), 16)
                value = jnp.concatenate([flip[j, base, :] for j in range(4)], axis=1)
                qsend[d, (i // 2) * 6 + s * 2 + i % 2] = value.astype(BF)
        return carry

    lax.fori_loop(0, 4, spread, 0)

    q_copies = []
    for g in range(4):
        for d in (1, 2, 3):
            part = pl.ds(g * 6, 6)
            copy = remote(qsend.at[zp[d], part], qrecv.at[z, part],
                          q_send.at[d, g], q_recv.at[d, g], (zp[d], c))
            copy.start()
            q_copies.append(copy)
    q_own = pltpu.make_async_copy(qsend.at[z], qrecv.at[z], q_send.at[0, 0])
    q_own.start()

    for da in (-1, 1):
        got("a", da)
    push(("a2", 0), -1, 0, 1, 0, 0)
    push(("a2", 1), 1, 0, -1, 0, 1)
    share(-1, 0)
    share(1, 0)
    for db in (-1, 1):
        got("b", 0, db)
        share(0, db)
    push(("b", -1, -1), -1, 0, 0, 1)
    push(("b", -1, 1), -1, 0, 0, -1)
    push(("b2", 0, 0), 0, -1, 0, 1, 0)
    push(("b2", 0, 1), 0, 1, 0, -1, 1)
    push(("b", 1, -1), 1, 0, 0, 1)

    @pl.when(cx == 0)
    def _():
        jump.wait_recv()
        jump_share.start()

    q_own.wait()

    def prefill_part(p, part, state):
        keys_up = upk[pl.ds(2 * p, 2)].reshape(256, DL)
        values_up = jnp.concatenate([upv[2 * p], upv[2 * p + 1]], axis=1)
        plain = qn[:, pl.ds(pl.multiple_of(p * 256, 256), 256)]
        turn = qr[:, pl.ds(pl.multiple_of(p * 128, 128), 128)]
        if part == 2:
            first = (cx == 0).astype(jnp.int32)
            older = lax.rem(c + 30, 32)
            newer = lax.rem(c + 31, 32)
            jumped = first * (1 - core)
            blocks = [older + first * (32 - older), newer + jumped * (33 - newer), c]
        else:
            blocks = [lax.rem(c - 8 + part * 3 + i + 32, 32) for i in range(3)]
        rows_here = jnp.concatenate(
            [allb[pl.ds(block * 4, 4)].reshape(256, KW) for block in blocks], axis=0)
        latent = rows_here[:, :DL]
        head_keys = nt(latent, keys_up).astype(BF)
        head_values = nn(latent, values_up).astype(BF)
        shut = bias[:, part * CHUNK:(part + 1) * CHUNK]
        following = []
        for e in range(2):
            query = jnp.concatenate([plain[:, e * 128:(e + 1) * 128], half_lanes(turn, e)], axis=1)
            key = jnp.concatenate([head_keys[:, e * 128:(e + 1) * 128], rows_here[:, DL:]], axis=1)
            value = jnp.concatenate(
                [head_values[:, e * 128:(e + 1) * 128], jnp.ones((CHUNK, 128), BF)], axis=1)
            score = nt(query, key) * SCALE + shut
            top = jnp.max(score, axis=1, keepdims=True)
            if state is None:
                weight = jnp.exp2(score - top)
                total = nn(weight.astype(BF), value)
            else:
                old_top, old_total = state[e]
                top = jnp.maximum(old_top, top)
                weight = jnp.exp2(score - top)
                total = old_total * jnp.exp2(old_top - top) + nn(weight.astype(BF), value)
            following.append((top, total))
        return following

    def prefill_near(p, carry):
        for e, (top, total) in enumerate(prefill_part(p, 2, None)):
            lane = lax.broadcasted_iota(jnp.int32, (256, 128), 1)
            tops[2 * p + e] = jnp.where(lane < 64, top, total[:, 128:])
            totals[2 * p + e] = total[:, :128]
        return carry

    def prefill_far(p, carry):
        state = []
        for e in range(2):
            known = tops[2 * p + e]
            summed = jnp.broadcast_to(known[:, 64:65], (256, 128))
            state.append((known[:, :1], jnp.concatenate([totals[2 * p + e], summed], axis=1)))
        for part in (1, 0):
            state = prefill_part(p, part, state)
        for e in range(2):
            total = state[e][1]
            pout[:, pl.ds(pl.multiple_of(p * 256 + e * 128, 128), 128)] = (
                total[:, :128] / total[:, 128:]).astype(BF)
        return carry

    for key in ((0, 0), (-1, 0), (0, -1)):
        got("s", *key)

    @pl.when(cx == 0)
    def _():
        jump_share.wait_recv()

    loads[9].wait()
    loads[10].wait()
    loads[11].wait()
    lax.fori_loop(0, 4, prefill_near, 0, unroll=2)
    got("a2", 0)
    got("a2", 1)
    push(("b", 2, -1), 2, 0, 0, 1)
    share(2, 0)
    got("b2", 0, 0)
    got("b2", 0, 1)
    share(0, 2)
    lax.fori_loop(4, 8, prefill_near, 0, unroll=2)
    got("b", -1, -1)
    got("b", -1, 1)
    push(("b2", -1, 0), -1, -1, 0, 1, 0)
    push(("b2", -1, 1), -1, 1, 0, -1, 1)
    share(-1, -1)
    share(-1, 1)
    got("b", 1, -1)
    share(1, -1)

    row_step = lax.rem(lax.div(lax.broadcasted_iota(jnp.int32, (192, 16), 0), 16), 3)
    fresh_col = lax.broadcasted_iota(jnp.int32, (192, 16), 1)
    fresh_seen = (fresh_col <= row_step) & (fresh_col < 3)

    def attend(queries, keys, used, recent):
        count = len(queries)
        new, scores, top = [], [[] for _ in range(count)], []
        for e in range(count):
            new.append(jnp.where(fresh_seen, nt(queries[e], recent[e]) * SCALE, NEG))
            top.append(jnp.max(new[e], axis=1, keepdims=True))
        for k in range(4):
            place = k * 512 + lax.broadcasted_iota(jnp.int32, (1, 512), 1)
            for e in range(count):
                part = nt(queries[e], keys(e, k)) * SCALE
                part = jnp.where(place < used[e], part, NEG)
                top[e] = jnp.maximum(top[e], jnp.max(part, axis=1, keepdims=True))
                scores[e].append(part)
        total, out = [], []
        for e in range(count):
            fresh_weight = jnp.exp2(new[e] - top[e])
            total.append(jnp.sum(fresh_weight, axis=1, keepdims=True))
            out.append(nn(fresh_weight.astype(BF), recent[e][:, :DL]))
        for k in range(4):
            for e in range(count):
                part = jnp.exp2(scores[e][k] - top[e])
                total[e] = total[e] + jnp.sum(part, axis=1, keepdims=True)
                out[e] = out[e] + nn(part.astype(BF), keys(e, k)[:, :DL])
        return [(out[e] / total[e]).astype(BF) for e in range(count)]

    def query_of(place, row):
        heads = [qrecv[o, place + 2 * s] for o in range(4) for s in range(3)]
        turns = [qrope[o, s * 8 + row] for o in range(4) for s in range(3)]
        return jnp.concatenate(
            [jnp.concatenate(heads, axis=0), jnp.concatenate(turns, axis=0)], axis=1)

    def decode_group(g):
        slots_here = [row_slot[0, 2 * g + e] for e in range(2)]

        def keys(e, k):
            found = []
            for r in range(8):
                page = jnp.minimum(pages[slots_here[e], k * 8 + r], 63)
                found.append(pool[page])
            return jnp.concatenate(found, axis=0)

        outs = attend(
            [query_of(6 * g + e, 2 * g + e) for e in range(2)], keys,
            [counts[slot] for slot in slots_here], [fresh[2 * g + e] for e in range(2)])
        for e in range(2):
            for o in range(4):
                for s in range(3):
                    obuf[o, 6 * g + 2 * s + e] = outs[e][(o * 3 + s) * 16:(o * 3 + s + 1) * 16]

    o_copies = []

    def send_out(first, count, g):
        part = pl.ds(first, count)
        for d in (1, 2, 3):
            copy = remote(obuf.at[zp[d], part], orecv.at[z, part],
                          o_send.at[d, g], o_recv.at[d, g], (zp[d], c))
            copy.start()
            o_copies.append(copy)

    for g in range(4):
        for d in range(3):
            q_copies[g * 3 + d].wait_recv()
        decode_group(g)
        send_out(6 * g, 6, g)
        if g == 1:
            got("b", 2, -1)
            share(2, -1)
            push(("b", 1, 1), 1, 0, 0, -1)
            push(("b", 2, 1), 2, 0, 0, -1)
        if g == 2:
            got("b2", -1, 0)
            got("b2", -1, 1)
            share(-1, 2)
    later = ((1, 1), (1, 2), (2, 1), (2, 2))
    for da in (0, -1, 1, 2):
        for db in (0, -1, 1, 2):
            if (da, db) not in later and (da, db) not in ((0, 0), (-1, 0), (0, -1)):
                got("s", da, db)
    lax.fori_loop(0, 2, prefill_far, 0, unroll=2)
    for da in (1, 2):
        got("b", da, 1)
        push(("b2", da, 0), da, -1, 0, 1, 0)
        push(("b2", da, 1), da, 1, 0, -1, 1)
        share(da, 1)
    lax.fori_loop(2, 4, prefill_far, 0, unroll=2)
    for da in (1, 2):
        got("b2", da, 0)
        got("b2", da, 1)
        share(da, 2)
    prefill_far(4, 0)
    for key in later:
        got("s", *key)

    device = z * 32 + c
    is_host = jnp.int32(0)
    arrival = jnp.int32(0)
    for r in range(8):
        hit = (hosts[r] == device).astype(jnp.int32)
        is_host = is_host + hit
        arrival = arrival + hit * lax.div(starts[r], PAGE)
    host_row = jnp.int32(0)
    for i in range(8):
        host_row = host_row + (row_slot[0, i] == 0).astype(jnp.int32) * i
    host_row = jnp.minimum(host_row, 7)

    def hosted_keys(e, k):
        found = []
        for r in range(8):
            page = jnp.minimum(arrival + k * 8 + r, 127)
            found.append(allb[page])
        return jnp.concatenate(found, axis=0)

    host_place = 6 * lax.div(host_row, 2) + lax.rem(host_row, 2)
    out = attend([query_of(host_place, host_row)], hosted_keys, [counts[0]], [fresh[host_row]])[0]
    for o in range(4):
        for s in range(3):
            obuf[o, 24 + s] = out[(o * 3 + s) * 16:(o * 3 + s + 1) * 16]
    send_out(24, 3, 4)

    early = 6
    prefill_far(5, 0)
    pout_copies = [
        pltpu.make_async_copy(pout.at[:, pl.ds(0, early * 256)], pout_h.at[:, pl.ds(0, early * 256)], out_sem.at[0])]
    pout_copies[0].start()

    o_own = pltpu.make_async_copy(obuf.at[z, pl.ds(0, 27)], orecv.at[z, pl.ds(0, 27)], o_send.at[0, 0])
    o_own.start()
    for d in range(4):
        orecv[d, 27:32] = jnp.zeros((5, 16, DL), BF)
    for copy in o_copies:
        copy.wait_recv()
    o_own.wait()

    def unspread(t, carry):
        for u in range(8):
            value = orecv[lax.div(t, 4), lax.rem(t, 4) * 8 + u].astype(F32)
            base = pl.ds(pl.multiple_of((t * 8 + u) * 16, 16), 16)
            for j in range(4):
                flip[j, base, :] = value[:, j * 128:(j + 1) * 128]
        return carry

    lax.fori_loop(0, 16, unspread, 0)

    def project(h, carry):
        value = jnp.concatenate([flip[j, pl.ds(h, 128, stride=16), :] for j in range(4)], axis=1)
        value = nn(value.astype(BF), upv[h]).astype(BF)
        for d in range(4):
            ysend[d, :, pl.ds(pl.multiple_of(h * 128, 128), 128)] = value[d * 32:(d + 1) * 32]
        return carry

    lax.fori_loop(0, 16, project, 0, unroll=4)
    y_copies = []
    for d in (1, 2, 3):
        copy = remote(ysend.at[zp[d]], yrecv.at[z], y_send.at[d], y_recv.at[d], (zp[d], c))
        copy.start()
        y_copies.append(copy)
    y_own = pltpu.make_async_copy(ysend.at[z], yrecv.at[z], y_send.at[0])
    y_own.start()

    lax.fori_loop(early, 8, prefill_far, 0, unroll=2)
    late = pl.ds(early * 256, 2048 - early * 256)
    pout_copies.append(pltpu.make_async_copy(pout.at[:, late], pout_h.at[:, late], out_sem.at[2]))
    pout_copies[1].start()
    y_own.wait()
    for copy in y_copies:
        copy.wait_recv()

    row = lax.broadcasted_iota(jnp.int32, (8, 32), 0)
    place = lax.broadcasted_iota(jnp.int32, (8, 32), 1)
    for s in range(3):
        source = jnp.where((row == host_row) & (is_host > 0), 24 + s, lax.div(row, 2) * 6 + s * 2 + lax.rem(row, 2))
        pick = (place == source).astype(F32).astype(BF)
        for d in range(4):
            dout[s, :, d * 2048:(d + 1) * 2048] = nn(pick, yrecv[d]).astype(BF)
    dout_copy = pltpu.make_async_copy(dout, dout_h, out_sem.at[1])
    dout_copy.start()

    for copy in z_copies + q_copies + o_copies + y_copies + list(gather.values()):
        copy.wait_send()

    @pl.when(cx == 3)
    def _():
        jump.wait_send()

    @pl.when(cx == 0)
    def _():
        jump_share.wait_send()

    for copy in pout_copies:
        copy.wait()
    dout_copy.wait()


def on_device(
    pre_q_nope, pre_q_rope, pre_latent, pre_rope, up_keys, up_values, new_lengths, new_hosts,
    req_pages, req_len, row_request, cache_latent, cache_rope, dec_q_nope, dec_q_rope,
    new_latent, new_rope,
):
    dma = pltpu.SemaphoreType.DMA
    vmem = pltpu.VMEM
    return pl.pallas_call(
        kernel,
        out_shape=(
            jax.ShapeDtypeStruct((256, 2048), BF),
            jax.ShapeDtypeStruct((3, 8, 8192), BF),
        ),
        in_specs=[pl.BlockSpec(memory_space=pltpu.SMEM)] * 5 + [pl.BlockSpec(memory_space=pl.ANY)] * 12,
        out_specs=[pl.BlockSpec(memory_space=pl.ANY)] * 2,
        scratch_shapes=[
            vmem((136, PAGE, KW), BF),
            vmem((DR, 256), BF),
            vmem((64, PAGE, KW), BF),
            vmem((DR, 4096), BF),
            vmem((16, DN, DL), BF),
            vmem((16, DL, DV), BF),
            vmem((256, 2048), BF),
            vmem((256, 1024), BF),
            vmem((256, 2048), BF),
            vmem((256, 2304), F32),
            vmem((4, 3, 8, 2048), BF),
            vmem((3, 8, 4096), BF),
            vmem((3, 8, DL), BF),
            vmem((3, 8, DR), BF),
            vmem((16, 256, 128), F32),
            vmem((16, 256, 128), F32),
            vmem((4, 2048, 128), F32),
            vmem((4, 24, 16, DL), BF),
            vmem((4, 24, 16, DL), BF),
            vmem((4, 24, 16, 128), BF),
            vmem((8, 16, KW), BF),
            vmem((4, 32, 16, DL), BF),
            vmem((4, 32, 16, DL), BF),
            vmem((4, 32, 2048), BF),
            vmem((4, 32, 2048), BF),
            vmem((3, 8, 8192), BF),
            dma((12,)),
            dma((4,)), dma((4,)),
            dma((4, 4)), dma((4, 4)),
            dma((4, 5)), dma((4, 5)),
            dma((4,)), dma((4,)),
            dma((36,)), dma((36,)),
            dma((2,)), dma((2,)),
            dma((3,)),
        ],
        compiler_params=pltpu.CompilerParams(
            collective_id=0, has_side_effects=True, vmem_limit_bytes=60 * 2**20),
        cost_estimate=pl.CostEstimate(flops=25 * 10**9, bytes_accessed=16 * 2**20, transcendentals=12 * 10**6),
    )(
        new_lengths, new_hosts, req_pages, req_len, row_request,
        pre_q_nope, pre_q_rope, pre_latent.reshape(4, PAGE, DL), pre_rope.T, up_keys, up_values,
        cache_latent.reshape(64, PAGE, DL), cache_rope.T, dec_q_nope, dec_q_rope, new_latent, new_rope,
    )


def solution(mesh):
    placed = (
        P("cp", "dp"),
        P("cp", "dp"),
        P("cp", None),
        P("cp", None),
        P("dp", None, None),
        P("dp", None, None),
        P(),
        P(),
        P(("dp", "cp"), None),
        P(("dp", "cp")),
        P(("dp", "cp"), None),
        P(("dp", "cp"), None),
        P(("dp", "cp"), None),
        P(None, ("dp", "cp"), None),
        P(None, ("dp", "cp"), None),
        P(None, ("dp", "cp"), None),
        P(None, ("dp", "cp"), None),
    )
    return jax.shard_map(
        on_device,
        mesh=mesh,
        in_specs=placed,
        out_specs=(P("cp", "dp"), P(None, ("dp", "cp"), None)),
        check_vma=False,
    )
```

```python
import jax
import jax.numpy as jnp
from jax import lax
from jax.experimental import pallas as pl
from jax.experimental.pallas import tpu as pltpu
from jax.sharding import PartitionSpec as P

DN, DR, DL, DV, PAGE = 128, 64, 512, 128, 64
F32, BF = jnp.float32, jnp.bfloat16
SCALE = (DN + DR) ** -0.5 * 1.4426950408889634
NEG = -1e30
KW = DL + 2 * DR
CHUNK = 768
MESH = pl.DeviceIdType.MESH


def nt(a, b):
    return lax.dot_general(a, b, (((1,), (1,)), ((), ())), preferred_element_type=F32)


def nn(a, b):
    return lax.dot_general(a, b, (((1,), (0,)), ((), ())), preferred_element_type=F32)


def half_lanes(pair, odd):
    lane = lax.broadcasted_iota(jnp.int32, pair.shape, 1)
    return jnp.where((lane >= DR) if odd else (lane < DR), pair, jnp.zeros_like(pair))


def kernel(
    lengths, hosts, pages, counts, row_slot,
    qn_h, qr_h, lat_h, rope_h, upk_h, upv_h, cl_h, cr_h, dq_h, dqr_h, nl_h, nr_h,
    pout_h, dout_h,
    allb, rope_st, pool, cr_st, upk, upv, qn, qr, pout, bias,
    qx, dqr, nl, nr, tops, totals, flip, qsend, qrecv, qrope, fresh, obuf, orecv, ysend, yrecv, dout,
    load_sem, z_send, z_recv, q_send, q_recv, o_send, o_recv, y_send, y_recv,
    a_send, a_recv, near_send, near_recv, out_sem,
):
    z = lax.axis_index("dp")
    c = lax.axis_index("cp")
    core = lax.rem(c, 2)
    chip = lax.div(c, 2)
    cx, cy = lax.rem(chip, 4), lax.div(chip, 4)
    a = cx + core * (cy - cx)
    b = cy + core * (cx - cy)

    def at(da, db):
        pa, pb = lax.rem(a + da + 4, 4), lax.rem(b + db + 4, 4)
        return 2 * (pa * (1 + 3 * core) + pb * (4 - 3 * core)) + core

    sibling = c + 1 - 2 * core
    zp = [lax.rem(z + d, 4) for d in range(4)]

    loads = [
        (lat_h, allb.at[pl.ds(4 * c, 4), :, pl.ds(0, DL)]),
        (rope_h, rope_st),
        (dq_h.at[:, :, pl.ds(pl.multiple_of(z * 2048, 2048), 2048)], qx.at[z]),
        (upk_h, upk),
        (dqr_h, dqr),
        (nl_h, nl),
        (nr_h, nr),
        (cl_h, pool.at[:, :, pl.ds(0, DL)]),
        (cr_h, cr_st),
        (qn_h, qn),
        (qr_h, qr),
        (upv_h, upv),
    ]
    loads = [pltpu.make_async_copy(s, d, load_sem.at[i]) for i, (s, d) in enumerate(loads)]
    for one in loads:
        one.start()

    barrier = pltpu.get_barrier_semaphore()
    peers = [(z, at(1, 0)), (z, at(-1, 0)), (z, at(0, 1)), (z, at(0, -1)), (z, sibling)]
    after, before = lax.rem(c + 2, 32), lax.rem(c + 30, 32)
    peers += [(zp[d], c) for d in (1, 2, 3)] + [(z, after), (z, before)]
    for peer in peers:
        pl.semaphore_signal(barrier, inc=1, device_id=peer, device_id_type=MESH)
    pl.semaphore_wait(barrier, len(peers))

    def remote(src, dst, send, recv, peer):
        return pltpu.make_async_remote_copy(
            src_ref=src, dst_ref=dst, send_sem=send, recv_sem=recv,
            device_id=peer, device_id_type=MESH)

    z_copies = []
    for d in (1, 2, 3):
        cols = pl.ds(pl.multiple_of(zp[d] * 2048, 2048), 2048)
        z_copies.append(remote(dq_h.at[:, :, cols], qx.at[z], z_send.at[d], z_recv.at[d], (zp[d], c)))
        z_copies[-1].start()

    loads[0].wait()
    loads[1].wait()
    own_rope = rope_st[...].astype(F32)
    own_rope = jnp.concatenate([own_rope, own_rope], axis=0).T
    allb[pl.ds(4 * c, 4), :, DL:] = own_rope.reshape(4, PAGE, 128).astype(BF)

    def rows(block, half=None):
        if half is None:
            return allb.at[pl.ds(block * 4, 4)]
        return allb.at[pl.ds(block * 4 + half * 2, 2)]

    near = [
        remote(rows(c), rows(32), near_send.at[0], near_recv.at[0], (z, after)),
        remote(rows(c), rows(33), near_send.at[1], near_recv.at[1], (z, sibling)),
        remote(rows(32), rows(34), near_send.at[2], near_recv.at[2], (z, sibling)),
    ]
    near[0].start()
    near[1].start()

    gather = {}
    slots = [0]

    def push(key, da, db, pa, pb, half=None):
        i = slots[0]
        slots[0] += 1
        ref = rows(at(da, db), half)
        copy = remote(ref, ref, a_send.at[i], a_recv.at[i], (z, at(pa, pb)))
        copy.start()
        gather[key] = copy

    def share(da, db):
        i = slots[0]
        slots[0] += 1
        ref = rows(at(da, db))
        copy = remote(ref, ref, a_send.at[i], a_recv.at[i], (z, sibling))
        copy.start()
        gather["s", da, db] = copy

    def got(*key):
        gather[key].wait_recv()

    push(("a", -1), 0, 0, 1, 0)
    push(("a", 1), 0, 0, -1, 0)
    push(("b", 0, -1), 0, 0, 0, 1)
    push(("b", 0, 1), 0, 0, 0, -1)
    share(0, 0)

    starts = [jnp.int32(0)]
    for r in range(7):
        starts.append(starts[-1] + lengths[r] * PAGE)
    query_pos = c * 256 + lax.broadcasted_iota(jnp.int32, (256, CHUNK), 0)
    low = jnp.zeros((256, CHUNK), jnp.int32)
    for r in range(1, 8):
        low = jnp.where(query_pos >= starts[r], starts[r], low)
    for part in range(3):
        key_pos = (c - 8) * 256 + part * CHUNK + lax.broadcasted_iota(jnp.int32, (256, CHUNK), 1)
        seen = (key_pos >= low) & (key_pos <= query_pos)
        bias[:, part * CHUNK:(part + 1) * CHUNK] = jnp.where(seen, 0.0, NEG)

    loads[4].wait()
    for owner in range(4):
        for pair in range(8):
            lanes = slice((owner * 8 + pair) * 128, (owner * 8 + pair + 1) * 128)
            value = jnp.concatenate([dqr[s, :, lanes].astype(F32) for s in range(3)], axis=0)
            for odd in range(2):
                flip[0, pl.ds(owner * 384 + pair * 2 + odd, 24, stride=16), :] = half_lanes(value, odd)
    for owner in range(4):
        qrope[owner] = flip[0, owner * 384:(owner + 1) * 384].reshape(24, 16, 128).astype(BF)

    loads[5].wait()
    loads[6].wait()
    for j in range(5):
        flip[j % 4, 0:128] = jnp.zeros((128, 128), F32)
        for s in range(3):
            if j < 4:
                value = nl[s, :, j * 128:(j + 1) * 128].astype(F32)
            else:
                value = nr[s].astype(F32)
                value = jnp.concatenate([value, value], axis=1)
            flip[j % 4, pl.ds(s, 8, stride=16), :] = value
        fresh[:, :, j * 128:(j + 1) * 128] = flip[j % 4, 0:128].reshape(8, 16, 128).astype(BF)

    loads[7].wait()
    loads[8].wait()
    for i in range(8):
        old_rope = cr_st[:, i * 512:(i + 1) * 512].astype(F32)
        old_rope = jnp.concatenate([old_rope, old_rope], axis=0).T
        pool[i * 8:(i + 1) * 8, :, DL:] = old_rope.reshape(8, PAGE, 128).astype(BF)

    near[0].wait_recv()
    near[2].start()

    loads[2].wait()
    loads[3].wait()
    for copy in z_copies:
        copy.wait_recv()

    def absorb(h, carry):
        lanes = pl.ds(pl.multiple_of(h * 128, 128), 128)
        value = jnp.concatenate(
            [qx[d, s, :, lanes].astype(F32) for d in range(4) for s in range(3)], axis=0)
        value = nn(value.astype(BF), upk[h])
        for j in range(4):
            flip[j, pl.ds(h, 96, stride=16), :] = value[:, j * 128:(j + 1) * 128]
        return carry

    lax.fori_loop(0, 16, absorb, 0, unroll=4)

    def spread(d, carry):
        for s in range(3):
            for i in range(8):
                base = pl.ds(pl.multiple_of((d * 24 + s * 8 + i) * 16, 16), 16)
                value = jnp.concatenate([flip[j, base, :] for j in range(4)], axis=1)
                qsend[d, (i // 2) * 6 + s * 2 + i % 2] = value.astype(BF)
        return carry

    lax.fori_loop(0, 4, spread, 0)

    q_copies = []
    for g in range(4):
        for d in (1, 2, 3):
            part = pl.ds(g * 6, 6)
            copy = remote(qsend.at[zp[d], part], qrecv.at[z, part],
                          q_send.at[d, g], q_recv.at[d, g], (zp[d], c))
            copy.start()
            q_copies.append(copy)
    q_own = pltpu.make_async_copy(qsend.at[z], qrecv.at[z], q_send.at[0, 0])
    q_own.start()

    got("a", -1)
    got("a", 1)
    push(("a2", 0), -1, 0, 1, 0, 0)
    push(("a2", 1), 1, 0, -1, 0, 1)
    for da in (-1, 1):
        push(("b", da, -1), da, 0, 0, 1)
        push(("b", da, 1), da, 0, 0, -1)
        share(da, 0)
    q_own.wait()

    def prefill_part(p, part, state):
        keys_up = upk[pl.ds(2 * p, 2)].reshape(256, DL)
        values_up = jnp.concatenate([upv[2 * p], upv[2 * p + 1]], axis=1)
        plain = qn[:, pl.ds(pl.multiple_of(p * 256, 256), 256)]
        turn = qr[:, pl.ds(pl.multiple_of(p * 128, 128), 128)]
        if part == 2:
            blocks = [32, 34 - core, c]
        else:
            blocks = [lax.rem(c - 8 + part * 3 + i + 32, 32) for i in range(3)]
        rows_here = jnp.concatenate(
            [allb[pl.ds(block * 4, 4)].reshape(256, KW) for block in blocks], axis=0)
        latent = rows_here[:, :DL]
        head_keys = nt(latent, keys_up).astype(BF)
        head_values = nn(latent, values_up).astype(BF)
        shut = bias[:, part * CHUNK:(part + 1) * CHUNK]
        following = []
        for e in range(2):
            query = jnp.concatenate([plain[:, e * 128:(e + 1) * 128], half_lanes(turn, e)], axis=1)
            key = jnp.concatenate([head_keys[:, e * 128:(e + 1) * 128], rows_here[:, DL:]], axis=1)
            value = jnp.concatenate(
                [head_values[:, e * 128:(e + 1) * 128], jnp.ones((CHUNK, 128), BF)], axis=1)
            score = nt(query, key) * SCALE + shut
            top = jnp.max(score, axis=1, keepdims=True)
            if state is None:
                weight = jnp.exp2(score - top)
                total = nn(weight.astype(BF), value)
            else:
                old_top, old_total = state[e]
                top = jnp.maximum(old_top, top)
                weight = jnp.exp2(score - top)
                total = old_total * jnp.exp2(old_top - top) + nn(weight.astype(BF), value)
            following.append((top, total))
        return following

    def prefill_near(p, carry):
        for e, (top, total) in enumerate(prefill_part(p, 2, None)):
            lane = lax.broadcasted_iota(jnp.int32, (256, 128), 1)
            tops[2 * p + e] = jnp.where(lane < 64, top, total[:, 128:])
            totals[2 * p + e] = total[:, :128]
        return carry

    def prefill_far(p, carry):
        state = []
        for e in range(2):
            known = tops[2 * p + e]
            summed = jnp.broadcast_to(known[:, 64:65], (256, 128))
            state.append((known[:, :1], jnp.concatenate([totals[2 * p + e], summed], axis=1)))
        for part in (1, 0):
            state = prefill_part(p, part, state)
        for e in range(2):
            total = state[e][1]
            pout[:, pl.ds(pl.multiple_of(p * 256 + e * 128, 128), 128)] = (
                total[:, :128] / total[:, 128:]).astype(BF)
        return carry

    near[1].wait_recv()
    near[2].wait_recv()
    loads[9].wait()
    loads[10].wait()
    loads[11].wait()
    lax.fori_loop(0, 4, prefill_near, 0, unroll=2)
    got("a2", 0)
    got("a2", 1)
    push(("b", 2, -1), 2, 0, 0, 1)
    push(("b", 2, 1), 2, 0, 0, -1)
    share(2, 0)
    got("b", 0, -1)
    got("b", 0, 1)
    push(("b2", 0, 0), 0, -1, 0, 1, 0)
    push(("b2", 0, 1), 0, 1, 0, -1, 1)
    share(0, -1)
    share(0, 1)
    lax.fori_loop(4, 8, prefill_near, 0, unroll=2)

    row_step = lax.rem(lax.div(lax.broadcasted_iota(jnp.int32, (192, 16), 0), 16), 3)
    fresh_col = lax.broadcasted_iota(jnp.int32, (192, 16), 1)
    fresh_seen = (fresh_col <= row_step) & (fresh_col < 3)

    def attend(queries, keys, used, recent):
        count = len(queries)
        new, scores, top = [], [[] for _ in range(count)], []
        for e in range(count):
            new.append(jnp.where(fresh_seen, nt(queries[e], recent[e]) * SCALE, NEG))
            top.append(jnp.max(new[e], axis=1, keepdims=True))
        for k in range(4):
            place = k * 512 + lax.broadcasted_iota(jnp.int32, (1, 512), 1)
            for e in range(count):
                part = nt(queries[e], keys(e, k)) * SCALE
                part = jnp.where(place < used[e], part, NEG)
                top[e] = jnp.maximum(top[e], jnp.max(part, axis=1, keepdims=True))
                scores[e].append(part)
        total, out = [], []
        for e in range(count):
            fresh_weight = jnp.exp2(new[e] - top[e])
            total.append(jnp.sum(fresh_weight, axis=1, keepdims=True))
            out.append(nn(fresh_weight.astype(BF), recent[e][:, :DL]))
        for k in range(4):
            for e in range(count):
                part = jnp.exp2(scores[e][k] - top[e])
                total[e] = total[e] + jnp.sum(part, axis=1, keepdims=True)
                out[e] = out[e] + nn(part.astype(BF), keys(e, k)[:, :DL])
        return [(out[e] / total[e]).astype(BF) for e in range(count)]

    def query_of(place, row):
        heads = [qrecv[o, place + 2 * s] for o in range(4) for s in range(3)]
        turns = [qrope[o, s * 8 + row] for o in range(4) for s in range(3)]
        return jnp.concatenate(
            [jnp.concatenate(heads, axis=0), jnp.concatenate(turns, axis=0)], axis=1)

    def decode_group(g):
        slots_here = [row_slot[0, 2 * g + e] for e in range(2)]

        def keys(e, k):
            found = []
            for r in range(8):
                page = jnp.minimum(pages[slots_here[e], k * 8 + r], 63)
                found.append(pool[page])
            return jnp.concatenate(found, axis=0)

        outs = attend(
            [query_of(6 * g + e, 2 * g + e) for e in range(2)], keys,
            [counts[slot] for slot in slots_here], [fresh[2 * g + e] for e in range(2)])
        for e in range(2):
            for o in range(4):
                for s in range(3):
                    obuf[o, 6 * g + 2 * s + e] = outs[e][(o * 3 + s) * 16:(o * 3 + s + 1) * 16]

    o_copies = []

    def send_out(first, count, g):
        part = pl.ds(first, count)
        for d in (1, 2, 3):
            copy = remote(obuf.at[zp[d], part], orecv.at[z, part],
                          o_send.at[d, g], o_recv.at[d, g], (zp[d], c))
            copy.start()
            o_copies.append(copy)

    for g in range(4):
        for d in range(3):
            q_copies[g * 3 + d].wait_recv()
        decode_group(g)
        send_out(6 * g, 6, g)
        if g == 0:
            for da in (-1, 1):
                got("b", da, -1)
                got("b", da, 1)
                push(("b2", da, 0), da, -1, 0, 1, 0)
                push(("b2", da, 1), da, 1, 0, -1, 1)
                share(da, -1)
                share(da, 1)
        if g == 1:
            got("b", 2, -1)
            got("b", 2, 1)
            push(("b2", 2, 0), 2, -1, 0, 1, 0)
            push(("b2", 2, 1), 2, 1, 0, -1, 1)
            share(2, -1)
            share(2, 1)
            got("b2", 0, 0)
            got("b2", 0, 1)
            share(0, 2)
        if g == 2:
            got("b2", -1, 0)
            got("b2", -1, 1)
            share(-1, 2)
    later = ((1, 2), (2, 2))
    for da in (0, -1, 1, 2):
        for db in (0, -1, 1, 2):
            if (da, db) not in later:
                got("s", da, db)
    lax.fori_loop(0, 4, prefill_far, 0, unroll=2)
    for da, db in later:
        got("b2", da, 0)
        got("b2", da, 1)
        share(da, db)
    for key in later:
        got("s", *key)

    device = z * 32 + c
    is_host = jnp.int32(0)
    arrival = jnp.int32(0)
    for r in range(8):
        hit = (hosts[r] == device).astype(jnp.int32)
        is_host = is_host + hit
        arrival = arrival + hit * lax.div(starts[r], PAGE)
    host_row = jnp.int32(0)
    for i in range(8):
        host_row = host_row + (row_slot[0, i] == 0).astype(jnp.int32) * i
    host_row = jnp.minimum(host_row, 7)

    def hosted_keys(e, k):
        found = []
        for r in range(8):
            page = jnp.minimum(arrival + k * 8 + r, 127)
            found.append(allb[page])
        return jnp.concatenate(found, axis=0)

    host_place = 6 * lax.div(host_row, 2) + lax.rem(host_row, 2)
    out = attend([query_of(host_place, host_row)], hosted_keys, [counts[0]], [fresh[host_row]])[0]
    for o in range(4):
        for s in range(3):
            obuf[o, 24 + s] = out[(o * 3 + s) * 16:(o * 3 + s + 1) * 16]
    send_out(24, 3, 4)

    early = 6
    lax.fori_loop(4, early, prefill_far, 0, unroll=2)
    pout_copies = [
        pltpu.make_async_copy(pout.at[:, pl.ds(0, early * 256)], pout_h.at[:, pl.ds(0, early * 256)], out_sem.at[0])]
    pout_copies[0].start()

    o_own = pltpu.make_async_copy(obuf.at[z, pl.ds(0, 27)], orecv.at[z, pl.ds(0, 27)], o_send.at[0, 0])
    o_own.start()
    for d in range(4):
        orecv[d, 27:32] = jnp.zeros((5, 16, DL), BF)
    for copy in o_copies:
        copy.wait_recv()
    o_own.wait()

    def unspread(t, carry):
        for u in range(8):
            value = orecv[lax.div(t, 4), lax.rem(t, 4) * 8 + u].astype(F32)
            base = pl.ds(pl.multiple_of((t * 8 + u) * 16, 16), 16)
            for j in range(4):
                flip[j, base, :] = value[:, j * 128:(j + 1) * 128]
        return carry

    lax.fori_loop(0, 16, unspread, 0)

    def project(h, carry):
        value = jnp.concatenate([flip[j, pl.ds(h, 128, stride=16), :] for j in range(4)], axis=1)
        value = nn(value.astype(BF), upv[h]).astype(BF)
        for d in range(4):
            ysend[d, :, pl.ds(pl.multiple_of(h * 128, 128), 128)] = value[d * 32:(d + 1) * 32]
        return carry

    lax.fori_loop(0, 16, project, 0, unroll=4)
    y_copies = []
    for d in (1, 2, 3):
        copy = remote(ysend.at[zp[d]], yrecv.at[z], y_send.at[d], y_recv.at[d], (zp[d], c))
        copy.start()
        y_copies.append(copy)
    y_own = pltpu.make_async_copy(ysend.at[z], yrecv.at[z], y_send.at[0])
    y_own.start()

    lax.fori_loop(early, 8, prefill_far, 0, unroll=2)
    late = pl.ds(early * 256, 2048 - early * 256)
    pout_copies.append(pltpu.make_async_copy(pout.at[:, late], pout_h.at[:, late], out_sem.at[2]))
    pout_copies[1].start()
    y_own.wait()
    for copy in y_copies:
        copy.wait_recv()

    row = lax.broadcasted_iota(jnp.int32, (8, 32), 0)
    place = lax.broadcasted_iota(jnp.int32, (8, 32), 1)
    for s in range(3):
        source = jnp.where((row == host_row) & (is_host > 0), 24 + s, lax.div(row, 2) * 6 + s * 2 + lax.rem(row, 2))
        pick = (place == source).astype(F32).astype(BF)
        for d in range(4):
            dout[s, :, d * 2048:(d + 1) * 2048] = nn(pick, yrecv[d]).astype(BF)
    dout_copy = pltpu.make_async_copy(dout, dout_h, out_sem.at[1])
    dout_copy.start()

    for copy in z_copies + q_copies + o_copies + y_copies + list(gather.values()):
        copy.wait_send()
    for copy in near:
        copy.wait_send()
    for copy in pout_copies:
        copy.wait()
    dout_copy.wait()


def on_device(
    pre_q_nope, pre_q_rope, pre_latent, pre_rope, up_keys, up_values, new_lengths, new_hosts,
    req_pages, req_len, row_request, cache_latent, cache_rope, dec_q_nope, dec_q_rope,
    new_latent, new_rope,
):
    dma = pltpu.SemaphoreType.DMA
    vmem = pltpu.VMEM
    return pl.pallas_call(
        kernel,
        out_shape=(
            jax.ShapeDtypeStruct((256, 2048), BF),
            jax.ShapeDtypeStruct((3, 8, 8192), BF),
        ),
        in_specs=[pl.BlockSpec(memory_space=pltpu.SMEM)] * 5 + [pl.BlockSpec(memory_space=pl.ANY)] * 12,
        out_specs=[pl.BlockSpec(memory_space=pl.ANY)] * 2,
        scratch_shapes=[
            vmem((140, PAGE, KW), BF),
            vmem((DR, 256), BF),
            vmem((64, PAGE, KW), BF),
            vmem((DR, 4096), BF),
            vmem((16, DN, DL), BF),
            vmem((16, DL, DV), BF),
            vmem((256, 2048), BF),
            vmem((256, 1024), BF),
            vmem((256, 2048), BF),
            vmem((256, 2304), F32),
            vmem((4, 3, 8, 2048), BF),
            vmem((3, 8, 4096), BF),
            vmem((3, 8, DL), BF),
            vmem((3, 8, DR), BF),
            vmem((16, 256, 128), F32),
            vmem((16, 256, 128), F32),
            vmem((4, 2048, 128), F32),
            vmem((4, 24, 16, DL), BF),
            vmem((4, 24, 16, DL), BF),
            vmem((4, 24, 16, 128), BF),
            vmem((8, 16, KW), BF),
            vmem((4, 32, 16, DL), BF),
            vmem((4, 32, 16, DL), BF),
            vmem((4, 32, 2048), BF),
            vmem((4, 32, 2048), BF),
            vmem((3, 8, 8192), BF),
            dma((12,)),
            dma((4,)), dma((4,)),
            dma((4, 4)), dma((4, 4)),
            dma((4, 5)), dma((4, 5)),
            dma((4,)), dma((4,)),
            dma((36,)), dma((36,)),
            dma((3,)), dma((3,)),
            dma((3,)),
        ],
        compiler_params=pltpu.CompilerParams(
            collective_id=0, has_side_effects=True, vmem_limit_bytes=60 * 2**20),
        cost_estimate=pl.CostEstimate(flops=25 * 10**9, bytes_accessed=16 * 2**20, transcendentals=12 * 10**6),
    )(
        new_lengths, new_hosts, req_pages, req_len, row_request,
        pre_q_nope, pre_q_rope, pre_latent.reshape(4, PAGE, DL), pre_rope.T, up_keys, up_values,
        cache_latent.reshape(64, PAGE, DL), cache_rope.T, dec_q_nope, dec_q_rope, new_latent, new_rope,
    )


def solution(mesh):
    placed = (
        P("cp", "dp"),
        P("cp", "dp"),
        P("cp", None),
        P("cp", None),
        P("dp", None, None),
        P("dp", None, None),
        P(),
        P(),
        P(("dp", "cp"), None),
        P(("dp", "cp")),
        P(("dp", "cp"), None),
        P(("dp", "cp"), None),
        P(("dp", "cp"), None),
        P(None, ("dp", "cp"), None),
        P(None, ("dp", "cp"), None),
        P(None, ("dp", "cp"), None),
        P(None, ("dp", "cp"), None),
    )
    return jax.shard_map(
        on_device,
        mesh=mesh,
        in_specs=placed,
        out_specs=(P("cp", "dp"), P(None, ("dp", "cp"), None)),
        check_vma=False,
    )
```
